32 devices in a mesh: slab: 2 (over y), date: 4 (over z), rng: 2 (over x), az: 2 (over core).
Axes of the slice: x: 2, y: 2, z: 4, core: 2. Of those that a mesh axis runs over, the one named last changes fastest.
Arguments:
- slc: bfloat16 [64, 2, 128, 512], P(('slab', 'date'), None, 'az', 'rng'), parts along dimension 0, may hold values from -30 to 30
- lags: int32 [32, 6], P('date'), may hold values from 0 to 8, as said below
Outputs:
- coherence: bfloat16 [64, 6, 128, 512], P(('slab', 'date'), None, 'az', 'rng'), parts along dimension 0
- log_ratio: bfloat16 [64, 6, 128, 512], P(('slab', 'date'), None, 'az', 'rng'), parts along dimension 0
- quegan: float32 [64, 128, 512], P(('slab', 'date'), 'az', 'rng'), parts along dimension 0
The draws below stay inside these ranges and needn't reach their ends.
There are 2 independent parts, one for each index of `slab`. The reference program is written for one: setup_inputs(seed, part) draws one part's arguments, and reference() takes and returns one part's arrays. A program takes and returns all parts, laid end to end along the dimension named above; an argument that names none is the same for every part. Nothing has to cross between parts.
Inputs may be any that keep to these rules, and one draw needn't show every extreme that they name: Each entry is 0 (no partner) or a lag with date + lag < 32; the nonzero lags of one date are distinct; date 0 lists 6 partners, one of them at lag 8.
All inputs are finite; a program needn't handle non-finite values.
Results may differ from the reference program's by a relative error of at most 0.012.
Values may be sent and summed in bfloat16 or wider, within the bound.
No kernel may reach another device: no remote copies, remote signals or barrier semaphores. Data moves between devices by JAX's collectives and lax.ppermute only.
A program may use at most 64 MiB of HBM per device.

```python
import jax
import jax.numpy as jnp
from jax import lax

SLOTS = 6
HALF_AZ = 2
HALF_RG = 10
LAG_MAX = 8
DATES = 32
LINES = 128
COLS = 512


def draw_slc(key, part):
    keys = jax.random.split(jax.random.fold_in(key, 11), 4)
    common = jnp.clip(jax.random.normal(keys[0], (1, 2, LINES, COLS), jnp.float32), -5.0, 5.0) * 0.7071
    own = jnp.clip(jax.random.normal(keys[1], (DATES, 2, LINES, COLS), jnp.float32), -5.0, 5.0) * 0.7071
    rho = jax.random.uniform(keys[2], (DATES, 1, 1, 1), jnp.float32, 0.3, 0.9)
    texture = jnp.exp(0.4 * jnp.clip(jax.random.normal(keys[3], (DATES, 1, LINES, COLS), jnp.float32), -3.0, 3.0))
    fields = texture * (jnp.sqrt(rho) * common + jnp.sqrt(1.0 - rho) * own)
    return jnp.clip(fields, -30.0, 30.0).astype(jnp.bfloat16)


def draw_lags(key, part):
    keys = jax.random.split(jax.random.fold_in(key, 23), 2)
    scores = jax.random.randint(keys[0], (DATES, LAG_MAX), 0, 1 << 20) * LAG_MAX + jnp.arange(LAG_MAX, dtype=jnp.int32)[None, :]
    order = jnp.argsort(scores, axis=1, stable=True)
    picked = (order[:, :SLOTS] + 1).astype(jnp.int32)
    counts = jax.random.randint(keys[1], (DATES, 1), 2, SLOTS + 1)
    slot_ids = jnp.arange(SLOTS, dtype=jnp.int32)[None, :]
    date_ids = jnp.arange(DATES, dtype=jnp.int32)[:, None]
    picked = jnp.where(date_ids == 0, LAG_MAX - slot_ids, picked)
    counts = jnp.where(date_ids == 0, SLOTS, counts)
    live_slots = (slot_ids < counts) & (date_ids + picked < DATES)
    return jnp.where(live_slots, picked, 0).astype(jnp.int32)


def setup_inputs(seed: int = 0, part: int = 0) -> dict:
    seeds = jax.random.split(jax.random.key(seed), 3)
    part_splits = jax.random.split(jax.random.fold_in(seeds[2], part), 3)
    return {
        "slc": draw_slc(jax.random.fold_in(jax.random.fold_in(seeds[2], part), 71), part),
        "lags": draw_lags(jax.random.fold_in(seeds[2], 71), part),
    }


EPS = 1e-5


def box_mean(fields):
    line_count = fields.shape[-2]
    column_count = fields.shape[-1]
    pad_width = [(0, 0)] * (fields.ndim - 2) + [(HALF_AZ, HALF_AZ), (HALF_RG, HALF_RG)]
    padded = jnp.pad(fields, pad_width)
    row_sums = padded[..., 0:line_count, :]
    for offset in range(1, 2 * HALF_AZ + 1):
        row_sums = row_sums + padded[..., offset:offset + line_count, :]
    totals = row_sums[..., :, 0:column_count]
    for offset in range(1, 2 * HALF_RG + 1):
        totals = totals + row_sums[..., :, offset:offset + column_count]
    return totals / float((2 * HALF_AZ + 1) * (2 * HALF_RG + 1))


def reference(slc, lags):
    fields = slc.astype(jnp.float32)
    powers = fields[:, 0] ** 2 + fields[:, 1] ** 2
    mean_power = lax.map(box_mean, powers) + EPS
    ratio_sum = jnp.sum(powers / mean_power, axis=0)
    quegan = mean_power * ratio_sum / float(DATES)

    def one_date(packed):
        date_index, lag_row = packed
        live_slots = lag_row > 0
        partners = (date_index + jnp.where(live_slots, lag_row, 0)).astype(jnp.int32)
        own_tile = fields[date_index]
        second = fields[partners]
        cross_re = own_tile[0][None] * second[:, 0] + own_tile[1][None] * second[:, 1]
        cross_im = own_tile[1][None] * second[:, 0] - own_tile[0][None] * second[:, 1]
        boxed_cross = box_mean(jnp.stack([cross_re, cross_im]))
        own_mean = mean_power[date_index][None]
        partner_mean = mean_power[partners]
        coherence = (boxed_cross[0] ** 2 + boxed_cross[1] ** 2) / (own_mean * partner_mean)
        log_ratio = jnp.log(own_mean / partner_mean)
        slot_mask = live_slots[:, None, None]
        return (jnp.where(slot_mask, coherence, 0.0).astype(jnp.bfloat16),
                jnp.where(slot_mask, log_ratio, 0.0).astype(jnp.bfloat16))

    coherence, log_ratio = lax.map(one_date, (jnp.arange(DATES, dtype=jnp.int32), lags))
    return coherence, log_ratio, quegan
```

```python
import jax
import jax.numpy as jnp
from jax import lax
from jax.experimental import pallas as pl
from jax.experimental.pallas import tpu as pltpu
from jax.sharding import PartitionSpec as P

HALF_AZ = 2
HALF_RG = 10
EPS = 1e-05
LOOKS = float((2 * HALF_AZ + 1) * (2 * HALF_RG + 1))

BF16 = jnp.bfloat16
F32 = jnp.float32
STRIP = 16
LANES = 128
GROUP = 4
CHUNKS = 2


def sides(axis, size, width):
    count = lax.axis_size(axis)
    me = lax.axis_index(axis)
    if count == 2:
        first = me == 0
        return [(jnp.where(first, size - width, 0), jnp.where(first, size, -width), [(0, 1), (1, 0)])]
    return [
        (size - width, -width, [(i, i + 1) for i in range(count - 1)]),
        (0, size, [(i + 1, i) for i in range(count - 1)]),
    ]


def marks(shape, where):
    row = lax.broadcasted_iota(jnp.int32, shape, 0)
    col = lax.broadcasted_iota(jnp.int32, shape, 1)
    return jnp.where(where(row, col), 1.0, 0.0).astype(BF16)


def dot(a, b, contract=(1, 0)):
    return lax.dot_general(a, b, (((contract[0],), (contract[1],)), ((), ())), preferred_element_type=F32)


class Sizes:
    def __init__(self, slc, lags):
        self.dates, _, self.lines, self.cols = slc.shape
        self.slots = lags.shape[1]
        self.images = 2 * self.dates
        self.az = 1 if lax.axis_size("az") == 2 else 2
        self.rng = 1 if lax.axis_size("rng") == 2 else 2
        self.rows = self.lines + STRIP
        self.width = self.cols + LANES
        self.slot_count = self.dates * self.slots
        per = self.dates // CHUNKS
        self.bounds = [(c * per, (c + 1) * per if c < CHUNKS - 1 else self.dates) for c in range(CHUNKS)]
        self.rim_rows = 0
        self.rim_cols = self.az * HALF_AZ * self.cols
        self.rim_corners = self.rim_cols + self.rng * self.images * self.lines
        self.rim_width = self.rim_corners + self.az * self.rng * LANES


def pack_kernel(z, x_ref, lags_ref, *out):
    lists_ref, count_ref = out[-2], out[-1]
    x = x_ref[...]
    az, rng = sides("az", z.lines, HALF_AZ), sides("rng", z.cols, HALF_RG)
    picks = []
    for j, (start, _, _) in enumerate(rng):
        pick = marks((STRIP, z.cols), lambda c, k: (k == start + c) & (c < HALF_RG))
        picks.append(pick)
        out[z.az + j][...] = dot(pick, x, (1, 1)).astype(BF16)
    for i, (start, _, _) in enumerate(az):
        pick = marks(
            (LANES, z.images * z.lines),
            lambda q, k: (k == (q % z.images) * z.lines + start + q // z.images) & (q < HALF_AZ * z.images),
        )
        edge = dot(pick, x).astype(BF16)
        for r in range(HALF_AZ):
            out[i][:, r * z.cols : (r + 1) * z.cols] = edge[r * z.images : (r + 1) * z.images]
        for j in range(z.rng):
            out[z.az + z.rng + i * z.rng + j][...] = dot(picks[j], edge, (1, 1)).astype(BF16)
    for n in range(2 + CHUNKS):
        count_ref[n] = 0
    for d in range(z.dates):
        for s in range(z.slots):
            lag = lags_ref[d, s]
            e = d + lag
            which = jnp.where(e < z.dates, 1, 2)
            for low, _ in z.bounds[1:]:
                which = which + jnp.where(e >= z.dates + low, 1, 0)
            which = jnp.where(lag > 0, which, 0)
            at = count_ref[which]
            lists_ref[which, at] = d * 65536 + s * 256 + e
            count_ref[which] = at + 1
    for n in range(2 + CHUNKS):
        lists_ref[n, z.slot_count] = count_ref[n]


def bands(z):
    az, rng = sides("az", z.lines, HALF_AZ), sides("rng", z.cols, HALF_RG)

    def across(k, o):
        at = jnp.where(k < z.cols, k, -(10**6))
        for j, (_, place, _) in enumerate(rng):
            c = k - z.cols - j * STRIP
            at = jnp.where((c >= 0) & (c < HALF_RG), place + c, at)
        return jnp.abs(at - o) <= HALF_RG

    def down(r, k):
        at = jnp.where(k < z.lines, k, -(10**6))
        for i, (_, place, _) in enumerate(az):
            c = k - z.lines - i * HALF_AZ
            at = jnp.where((c >= 0) & (c < HALF_AZ), place + c, at)
        return jnp.abs(at - r) <= HALF_AZ

    columns = marks((z.width, z.cols), across)
    lines = marks((z.lines, z.rows), down)
    both = marks(
        (2 * z.lines, 2 * z.rows),
        lambda r, k: ((r < z.lines) & (k < z.rows) & down(r, k))
        | ((r >= z.lines) & (k >= z.rows) & down(r - z.lines, k - z.rows)),
    )
    return columns, lines, both


def assemble(z, tile_ref, x_ref, rim_ref, first, number):
    tile_ref[:, : z.lines, : z.cols] = x_ref[...].reshape(number, z.lines, z.cols)
    edge = jnp.zeros((number * STRIP, z.cols), F32)
    for i in range(z.az):
        for r in range(HALF_AZ):
            put = marks(
                (number * STRIP, z.images),
                lambda p, k: (k == first + p // STRIP) & (p % STRIP == i * HALF_AZ + r),
            )
            at = (i * HALF_AZ + r) * z.cols
            edge = edge + dot(put, rim_ref[: z.images, at : at + z.cols])
    tile_ref[:, z.lines :, : z.cols] = edge.astype(BF16).reshape(number, STRIP, z.cols)
    side = jnp.zeros((number * z.lines, LANES), F32)
    corner = jnp.zeros((number * STRIP, LANES), F32)
    for j in range(z.rng):
        spread = marks((STRIP, LANES), lambda c, lane: lane == c + j * STRIP)
        at = z.rim_cols + (j * z.images + first) * z.lines
        side = side + dot(rim_ref[:STRIP, at : at + number * z.lines], spread, (0, 0))
        for i in range(z.az):
            at = z.rim_corners + (i * z.rng + j) * LANES
            turned = dot(rim_ref[:STRIP, at : at + LANES], spread, (0, 0)).astype(BF16)
            put = marks(
                (number * STRIP, LANES),
                lambda p, q: (q % z.images == first + p // STRIP)
                & (p % STRIP == i * HALF_AZ + q // z.images)
                & (q < HALF_AZ * z.images),
            )
            corner = corner + dot(put, turned)
    tile_ref[:, : z.lines, z.cols :] = side.astype(BF16).reshape(number, z.lines, LANES)
    tile_ref[:, z.lines :, z.cols :] = corner.astype(BF16).reshape(number, STRIP, LANES)


def split(x):
    high = x.astype(BF16)
    return high, (x - high.astype(F32)).astype(BF16)


def look_stats(z, re, im, columns, lines):
    re, im = re.astype(F32), im.astype(F32)
    power = re * re + im * im
    sums = dot(jnp.concatenate(split(power), axis=0), columns)
    high, low = split(sums[: z.rows] + sums[z.rows :])
    mean = (dot(lines, high) + dot(lines, low)) * (1.0 / LOOKS) + EPS
    return power[: z.lines, : z.cols], mean, 1.0 / mean


def do_pairs(z, own, other, other_base, own_inv, own_log, other_inv, other_log, columns, both, lists, row, coh, log, stage_coh, stage_log, sems):
    count = lists[row, z.slot_count]

    def copies(k):
        code = lists[row, k]
        d, s = code // 65536, (code // 256) % 256
        return (
            pltpu.make_async_copy(stage_coh.at[k], coh.at[d, s], sems.at[0, k]),
            pltpu.make_async_copy(stage_log.at[k], log.at[d, s], sems.at[1, k]),
        )

    def group(step, _):
        first = step * GROUP
        picks, products = [], []
        for g in range(GROUP):
            k = jnp.minimum(first + g, count - 1)
            code = lists[row, k]
            d, e = code // 65536, code % 256 - other_base
            picks.append((k, d, e))
            a0, a1 = own[2 * d], own[2 * d + 1]
            b0, b1 = other[2 * e], other[2 * e + 1]
            products += [a0 * b0 + a1 * b1, a1 * b0 - a0 * b1]
        sums = dot(jnp.concatenate(products, axis=0), columns).astype(BF16)
        for g, (k, d, e) in enumerate(picks):
            boxed = dot(both, sums[g * 2 * z.rows : (g + 1) * 2 * z.rows])
            re, im = boxed[: z.lines], boxed[z.lines :]
            stage_coh[k] = ((re * re + im * im) * (own_inv[d] * other_inv[e])).astype(BF16)
            stage_log[k] = (own_log[d] - other_log[e]).astype(BF16)
        for g in range(GROUP):

            @pl.when(first + g < count)
            def _():
                for copy in copies(first + g):
                    copy.start()

        return 0

    lax.fori_loop(0, (count + GROUP - 1) // GROUP, group, 0)

    def finish(k, _):
        for copy in copies(k):
            copy.wait()
        return 0

    return lambda: lax.fori_loop(0, count, finish, 0)


def own_kernel(z, x_ref, rim_ref, lists, tile_ref, mean_ref, inv_ref, log_ref, part_ref, coh, logr, stage_coh, stage_log, zeros, sems, zero_sems):
    zeros[...] = jnp.zeros_like(zeros)
    dead = lists[0, z.slot_count]

    def dead_copies(k):
        code = lists[0, k]
        d, s = code // 65536, (code // 256) % 256
        return (
            pltpu.make_async_copy(zeros, coh.at[d, s], zero_sems.at[0, k]),
            pltpu.make_async_copy(zeros, logr.at[d, s], zero_sems.at[1, k]),
        )

    def clear(k, _):
        for copy in dead_copies(k):
            copy.start()
        return 0

    lax.fori_loop(0, dead, clear, 0)
    columns, lines, both = bands(z)
    assemble(z, tile_ref, x_ref, rim_ref, 0, z.images)

    def date(d, part):
        power, mean, inv = look_stats(z, tile_ref[2 * d], tile_ref[2 * d + 1], columns, lines)
        mean_ref[d] = mean
        inv_ref[d] = inv * (1.0 / LOOKS)
        log_ref[d] = jnp.log(mean)
        return part + power * inv

    part = lax.fori_loop(0, z.dates, date, jnp.zeros((z.lines, z.cols), F32), unroll=2)
    part_ref[...] = part.astype(BF16)
    done = do_pairs(z, tile_ref, tile_ref, 0, inv_ref, log_ref, inv_ref, log_ref, columns, both, lists, 1, coh, logr, stage_coh, stage_log, sems)
    done()

    def cleared(k, _):
        for copy in dead_copies(k):
            copy.wait()
        return 0

    lax.fori_loop(0, dead, cleared, 0)


def cross_kernel(z, chunk, dates_total, parts, x_ref, rim_ref, lists, own, mean_ref, inv_ref, log_ref, *rest):
    part_refs, rest = rest[:parts], rest[parts + 2 :]
    if parts:
        quegan, rest = rest[0], rest[1:]
    coh, logr, tile, other_inv, other_log, stage_coh, stage_log, sems = rest[:8]
    low, high = z.bounds[chunk]
    if parts:
        stage_q, q_sem = rest[8:]
        total = part_refs[0][...].astype(F32)
        for ref in part_refs[1:]:
            total = total + ref[...].astype(F32)
        total = total * (1.0 / dates_total)
        for d in range(z.dates):
            stage_q[d] = mean_ref[d] * total
        q_copy = pltpu.make_async_copy(stage_q, quegan, q_sem)
        q_copy.start()
    columns, lines, both = bands(z)
    assemble(z, tile, x_ref, rim_ref, 2 * low, 2 * (high - low))

    def date(d, _):
        _, mean, inv = look_stats(z, tile[2 * d], tile[2 * d + 1], columns, lines)
        other_inv[d] = inv * (1.0 / LOOKS)
        other_log[d] = jnp.log(mean)
        return 0

    lax.fori_loop(0, high - low, date, 0, unroll=2)
    done = do_pairs(z, own, tile, z.dates + low, inv_ref, log_ref, other_inv, other_log, columns, both, lists, 2 + chunk, coh, logr, stage_coh, stage_log, sems)
    done()
    if parts:
        q_copy.wait()


def vmem(n):
    return [pl.BlockSpec(memory_space=pltpu.VMEM)] * n


SMEM = pl.BlockSpec(memory_space=pltpu.SMEM)
HBM = pl.BlockSpec(memory_space=pltpu.HBM)
PARAMS = pltpu.CompilerParams(vmem_limit_bytes=50 * 1024 * 1024)


def on_device(slc, lags):
    z = Sizes(slc, lags)
    shape = jax.ShapeDtypeStruct
    flat = slc.reshape(z.images * z.lines, z.cols)
    count = lax.axis_size("date")
    earlier = [(i, i - 1) for i in range(1, count)]
    later = [
        lax.ppermute(flat[2 * low * z.lines : 2 * high * z.lines], "date", earlier) for low, high in z.bounds
    ]

    packed = pl.pallas_call(
        lambda *refs: pack_kernel(z, *refs),
        out_shape=[shape((STRIP, HALF_AZ * z.cols), BF16)] * z.az
        + [shape((STRIP, z.images * z.lines), BF16)] * z.rng
        + [shape((STRIP, LANES), BF16)] * (z.az * z.rng)
        + [shape((2 + CHUNKS, z.slot_count + 1), jnp.int32)],
        in_specs=vmem(1) + [SMEM],
        out_specs=vmem(z.az + z.rng + z.az * z.rng) + [SMEM],
        scratch_shapes=[pltpu.SMEM((2 + CHUNKS,), jnp.int32)],
        compiler_params=PARAMS,
        name="pack",
    )(flat, lags)
    lists = packed[-1]
    az, rng = sides("az", z.lines, HALF_AZ), sides("rng", z.cols, HALF_RG)
    rim = [lax.ppermute(packed[i], "az", az[i][2]) for i in range(z.az)]
    rim += [lax.ppermute(packed[z.az + j], "rng", rng[j][2]) for j in range(z.rng)]
    for i in range(z.az):
        for j in range(z.rng):
            corner = lax.ppermute(packed[z.az + z.rng + i * z.rng + j], "az", az[i][2])
            rim.append(lax.ppermute(corner, "rng", rng[j][2]))
    rim = jnp.concatenate(rim, axis=1)
    later_rim = lax.ppermute(rim, "date", earlier)

    field = shape((z.dates, z.lines, z.cols), F32)
    out = shape((z.dates, z.slots, z.lines, z.cols), BF16)
    stage = pltpu.VMEM((z.slot_count, z.lines, z.cols), BF16)
    sems = pltpu.SemaphoreType.DMA((2, z.slot_count))
    own, mean, inv, log, part, coherence, log_ratio = pl.pallas_call(
        lambda *refs: own_kernel(z, *refs),
        out_shape=[shape((z.images, z.rows, z.width), BF16), field, field, field, shape((z.lines, z.cols), BF16), out, out],
        in_specs=vmem(2) + [SMEM],
        out_specs=vmem(5) + [HBM] * 2,
        scratch_shapes=[stage, stage, pltpu.VMEM((z.lines, z.cols), BF16), sems, sems],
        compiler_params=PARAMS,
        name="own",
    )(flat, rim, lists)

    if count & (count - 1) == 0 and count <= 4:
        parts = [part] + [lax.ppermute(part, "date", [(i, i ^ k) for i in range(count)]) for k in range(1, count)]
    else:
        parts = [lax.psum(part, "date")]

    for chunk, (low, high) in enumerate(z.bounds):
        last = chunk == len(z.bounds) - 1
        extra = parts if last else []
        number = high - low
        other = pltpu.VMEM((number, z.lines, z.cols), F32)
        results = pl.pallas_call(
            lambda *refs, chunk=chunk, n=len(extra): cross_kernel(z, chunk, z.dates * count, n, *refs),
            out_shape=([field] if last else []) + [out, out],
            in_specs=vmem(2) + [SMEM] + vmem(4 + len(extra)) + [HBM] * 2,
            out_specs=([HBM] if last else []) + [HBM] * 2,
            scratch_shapes=[pltpu.VMEM((2 * number, z.rows, z.width), BF16), other, other, stage, stage, sems]
            + ([pltpu.VMEM(field.shape, F32), pltpu.SemaphoreType.DMA] if last else []),
            input_output_aliases={7 + len(extra): 1 if last else 0, 8 + len(extra): 2 if last else 1},
            compiler_params=PARAMS,
            name="cross",
        )(later[chunk], later_rim, lists, own, mean, inv, log, *extra, coherence, log_ratio)
        coherence, log_ratio = results[-2:]
    return coherence, log_ratio, results[0]


def solution(mesh):
    return jax.shard_map(
        on_device,
        mesh=mesh,
        in_specs=(P(("slab", "date"), None, "az", "rng"), P("date", None)),
        out_specs=(
            P(("slab", "date"), None, "az", "rng"),
            P(("slab", "date"), None, "az", "rng"),
            P(("slab", "date"), "az", "rng"),
        ),
        check_vma=False,
    )
```

```python
import jax
import jax.numpy as jnp
from jax import lax
from jax.experimental import pallas as pl
from jax.experimental.pallas import tpu as pltpu
from jax.sharding import PartitionSpec as P

HALF_AZ = 2
HALF_RG = 10
EPS = 1e-05
LOOKS = float((2 * HALF_AZ + 1) * (2 * HALF_RG + 1))

BF16 = jnp.bfloat16
F32 = jnp.float32
STRIP = 16
LANES = 128
GROUP = 4
CHUNKS = 1


def sides(axis, size, width):
    count = lax.axis_size(axis)
    me = lax.axis_index(axis)
    if count == 2:
        first = me == 0
        return [(jnp.where(first, size - width, 0), jnp.where(first, size, -width), [(0, 1), (1, 0)])]
    return [
        (size - width, -width, [(i, i + 1) for i in range(count - 1)]),
        (0, size, [(i + 1, i) for i in range(count - 1)]),
    ]


def marks(shape, where):
    row = lax.broadcasted_iota(jnp.int32, shape, 0)
    col = lax.broadcasted_iota(jnp.int32, shape, 1)
    return jnp.where(where(row, col), 1.0, 0.0).astype(BF16)


def dot(a, b, contract=(1, 0)):
    return lax.dot_general(a, b, (((contract[0],), (contract[1],)), ((), ())), preferred_element_type=F32)


class Sizes:
    def __init__(self, slc, lags):
        self.dates, _, self.lines, self.cols = slc.shape
        self.slots = lags.shape[1]
        self.images = 2 * self.dates
        self.az = 1 if lax.axis_size("az") == 2 else 2
        self.rng = 1 if lax.axis_size("rng") == 2 else 2
        self.rows = self.lines + STRIP
        self.width = self.cols + LANES
        self.slot_count = self.dates * self.slots
        per = self.dates // CHUNKS
        self.bounds = [(c * per, (c + 1) * per if c < CHUNKS - 1 else self.dates) for c in range(CHUNKS)]
        self.rim_rows = 0
        self.rim_cols = self.az * HALF_AZ * self.cols
        self.rim_corners = self.rim_cols + self.rng * self.images * self.lines
        self.rim_width = self.rim_corners + self.az * self.rng * LANES


def make_lists(z, lags_ref, lists_ref, count_ref):
    for n in range(2 + CHUNKS):
        count_ref[n] = 0
    for d in range(z.dates):
        for s in range(z.slots):
            lag = lags_ref[d, s]
            e = d + lag
            which = jnp.where(e < z.dates, 1, 2)
            for low, _ in z.bounds[1:]:
                which = which + jnp.where(e >= z.dates + low, 1, 0)
            which = jnp.where(lag > 0, which, 0)
            at = count_ref[which]
            lists_ref[which, at] = d * 65536 + s * 256 + e
            count_ref[which] = at + 1
    for n in range(2 + CHUNKS):
        lists_ref[n, z.slot_count] = count_ref[n]


def places(z, axis, k, inside, tail, unit, width):
    at = jnp.where(k < inside, k, -(10**6))
    for j, (_, place, _) in enumerate(sides(axis, inside, width)):
        c = k - tail - j * unit
        at = jnp.where((c >= 0) & (c < width), place + c, at)
    return at


def near(a, b, reach):
    return jnp.where(jnp.abs(a - b) <= reach, 1.0, 0.0).astype(BF16)


def make_bands(z, columns_ref):
    at = places(z, "rng", lax.broadcasted_iota(jnp.int32, (z.width, 1), 0), z.cols, z.cols, STRIP, HALF_RG)
    columns_ref[...] = near(at, lax.broadcasted_iota(jnp.int32, (z.width, z.cols), 1), HALF_RG)


def pack_kernel(z, slc_ref, *out):
    x = slc_ref[...]
    out[z.az + z.rng][...] = x
    az, rng = sides("az", z.lines, HALF_AZ), sides("rng", z.cols, HALF_RG)
    picks = [marks((STRIP, z.cols), lambda c, k: (k == start + c) & (c < HALF_RG)) for start, _, _ in rng]
    for i, (start, _, _) in enumerate(az):
        q = lax.broadcasted_iota(jnp.int32, (LANES, 1), 0)
        wanted = jnp.where(q < HALF_AZ * z.images, (q % z.images) * z.lines + start + q // z.images, -1)
        edge = dot(near(wanted, lax.broadcasted_iota(jnp.int32, (LANES, z.images * z.lines), 1), 0), x).astype(BF16)
        for r in range(HALF_AZ):
            out[i][:, r * z.cols : (r + 1) * z.cols] = edge[r * z.images : (r + 1) * z.images]
        for j, pick in enumerate(picks):
            at = z.images * z.lines + i * LANES
            out[z.az + j][:, at : at + LANES] = dot(pick, edge, (1, 1)).astype(BF16)
    for j, pick in enumerate(picks):
        out[z.az + j][:, : z.images * z.lines] = dot(pick, x, (1, 1)).astype(BF16)


def prepare_kernel(z, lags_ref, columns_ref, lists_ref, lags_s, lists_s, count_s, sem):
    take = pltpu.make_async_copy(lags_ref, lags_s, sem)
    take.start()
    make_bands(z, columns_ref)
    take.wait()
    make_lists(z, lags_s, lists_s, count_s)
    give = pltpu.make_async_copy(lists_s, lists_ref, sem)
    give.start()
    give.wait()


def assemble(z, tile_ref, x_ref, rim_ref, first, number):
    tile_ref[:, STRIP:, : z.cols] = x_ref[...].reshape(number, z.lines, z.cols)
    p = lax.broadcasted_iota(jnp.int32, (number * STRIP, 1), 0)
    az = [jnp.where(place < 0, STRIP + place, 0) for _, place, _ in sides("az", z.lines, HALF_AZ)]
    edge = jnp.zeros((number * STRIP, z.cols), F32)
    for i in range(z.az):
        for r in range(HALF_AZ):
            wanted = jnp.where(p % STRIP == az[i] + r, first + p // STRIP, -1)
            put = near(wanted, lax.broadcasted_iota(jnp.int32, (number * STRIP, z.images), 1), 0)
            at = (i * HALF_AZ + r) * z.cols
            edge = edge + dot(put, rim_ref[: z.images, at : at + z.cols])
    tile_ref[:, :STRIP, : z.cols] = edge.astype(BF16).reshape(number, STRIP, z.cols)
    side = jnp.zeros((number * z.lines, LANES), F32)
    corner = jnp.zeros((number * STRIP, LANES), F32)
    for j in range(z.rng):
        spread = marks((STRIP, LANES), lambda c, lane: lane == c + j * STRIP)
        at = z.rim_cols + (j * z.images + first) * z.lines
        side = side + dot(rim_ref[:STRIP, at : at + number * z.lines], spread, (0, 0))
        for i in range(z.az):
            at = z.rim_corners + (i * z.rng + j) * LANES
            turned = dot(rim_ref[:STRIP, at : at + LANES], spread, (0, 0)).astype(BF16)
            r = p % STRIP - az[i]
            wanted = jnp.where((r >= 0) & (r < HALF_AZ), r * z.images + first + p // STRIP, -1)
            put = near(wanted, lax.broadcasted_iota(jnp.int32, (number * STRIP, LANES), 1), 0)
            corner = corner + dot(put, turned)
    tile_ref[:, STRIP:, z.cols :] = side.astype(BF16).reshape(number, z.lines, LANES)
    tile_ref[:, :STRIP, z.cols :] = corner.astype(BF16).reshape(number, STRIP, LANES)


def split(x):
    high = x.astype(BF16)
    return high, (x - high.astype(F32)).astype(BF16)


def down_sums(z, x):
    half = STRIP // 2
    x = jnp.concatenate([x[half:], x[:half]], axis=0)
    top = half - HALF_AZ
    twos = x[top : top + z.lines + 3] + x[top + 1 : top + z.lines + 4]
    fours = twos[: z.lines + 1] + twos[2 : z.lines + 3]
    return fours[: z.lines] + x[half + HALF_AZ : half + HALF_AZ + z.lines]


def look_stats(z, tile, first, number, columns):
    powers, parts = [], []
    for d in range(first, first + number):
        re, im = tile[2 * d].astype(F32), tile[2 * d + 1].astype(F32)
        power = re * re + im * im
        powers.append(power[STRIP:, : z.cols])
        parts += split(power)
    sums = dot(jnp.concatenate(parts, axis=0), columns)
    for n, power in enumerate(powers):
        at = 2 * n * z.rows
        both = sums[at : at + z.rows] + sums[at + z.rows : at + 2 * z.rows]
        mean = down_sums(z, both) * (1.0 / LOOKS) + EPS
        yield first + n, power, mean, 1.0 / mean


def do_pairs(z, own, other, other_base, own_inv, own_log, other_inv, other_log, columns, lists, row, coh, log, stage_coh, stage_log, sums, sem):
    count = lists[row, z.slot_count]
    steps = (count + GROUP - 1) // GROUP

    def pick(step, g):
        k = jnp.minimum(step * GROUP + g, count - 1)
        code = lists[row, k]
        return k, code // 65536, code % 256 - other_base

    def copies(k):
        code = lists[row, k]
        d, s = code // 65536, (code // 256) % 256
        return (
            pltpu.make_async_copy(stage_coh.at[k], coh.at[d, s], sem),
            pltpu.make_async_copy(stage_log.at[k], log.at[d, s], sem),
        )

    def across(step, slot):
        products = []
        for g in range(GROUP):
            _, d, e = pick(step, g)
            a0, a1 = own[2 * d], own[2 * d + 1]
            b0, b1 = other[2 * e], other[2 * e + 1]
            products += [a0 * b0 + a1 * b1, a1 * b0 - a0 * b1]
        sums[slot] = dot(jnp.concatenate(products, axis=0), columns)

    def down(step, slot):
        for g in range(GROUP):
            k, d, e = pick(step, g)
            re = down_sums(z, sums[slot, 2 * g * z.rows : (2 * g + 1) * z.rows])
            im = down_sums(z, sums[slot, (2 * g + 1) * z.rows : (2 * g + 2) * z.rows])
            stage_coh[k] = ((re * re + im * im) * (own_inv[d] * other_inv[e])).astype(BF16)
            stage_log[k] = (own_log[d] - other_log[e]).astype(BF16)

    @pl.when(count > 0)
    def _():
        across(0, 0)

    def group(step, _):
        for slot in range(2):

            @pl.when(step % 2 == slot)
            def _():
                down(step, slot)
                across(step + 1, 1 - slot)

        for g in range(GROUP):

            @pl.when(step * GROUP + g < count)
            def _():
                for copy in copies(step * GROUP + g):
                    copy.start()

        return 0

    lax.fori_loop(0, steps, group, 0)

    def finish(k, _):
        for copy in copies(k):
            copy.wait()
        return 0

    return lambda: lax.fori_loop(0, count, finish, 0)


def stats_kernel(z, x_ref, rim_ref, columns, tile_ref, mean_ref, inv_ref, log_ref, part_ref, bundle_ref):
    assemble(z, tile_ref, x_ref, rim_ref, 0, z.images)
    part = jnp.zeros((z.lines, z.cols), F32)
    for first in range(0, z.dates, GROUP):
        for d, power, mean, inv in look_stats(z, tile_ref, first, min(GROUP, z.dates - first), columns[...]):
            mean_ref[d] = mean
            inv_ref[d] = inv * (1.0 / LOOKS)
            log_ref[d] = jnp.log(mean)
            part = part + power * inv
    part = part.astype(BF16)
    part_ref[...] = part
    bundle_ref[:, : z.rim_width] = rim_ref[...]
    for i in range(z.lines // STRIP):
        at = z.rim_width + i * z.cols
        bundle_ref[:STRIP, at : at + z.cols] = part[i * STRIP : (i + 1) * STRIP]


def own_kernel(z, lists_ref, columns, tile, inv, log, coh, logr, stage_coh, stage_log, sums, zeros, lists, sems):
    take = pltpu.make_async_copy(lists_ref, lists, sems.at[0])
    take.start()
    zeros[...] = jnp.zeros_like(zeros)
    take.wait()
    dead = lists[0, z.slot_count]

    def dead_copies(k):
        code = lists[0, k]
        d, s = code // 65536, (code // 256) % 256
        return (
            pltpu.make_async_copy(zeros, coh.at[d, s], sems.at[1]),
            pltpu.make_async_copy(zeros, logr.at[d, s], sems.at[1]),
        )

    def clear(k, _):
        for copy in dead_copies(k):
            copy.start()
        return 0

    lax.fori_loop(0, dead, clear, 0)
    done = do_pairs(z, tile, tile, 0, inv, log, inv, log, columns[...], lists, 1, coh, logr, stage_coh, stage_log, sums, sems.at[0])
    done()

    def cleared(k, _):
        for copy in dead_copies(k):
            copy.wait()
        return 0

    lax.fori_loop(0, dead, cleared, 0)


def cross_kernel(z, chunk, dates_total, parts, x_ref, rim_ref, lists_ref, columns, own, inv_ref, log_ref, *rest):
    if parts:
        mean, rest = rest[0], rest[1:]
    part_refs, rest = rest[:parts], rest[parts + 2 :]
    if parts:
        quegan, rest = rest[0], rest[1:]
    coh, logr, tile, other_inv, other_log, stage_coh, stage_log, sums, lists, sems = rest[:10]
    take = pltpu.make_async_copy(lists_ref, lists, sems.at[0])
    take.start()
    low, high = z.bounds[chunk]
    if parts:
        stage_q = rest[10]
        total = part_refs[0][...].astype(F32)
        for ref in part_refs[1:]:
            total = total + ref[...].astype(F32)
        if parts > 1:
            ats = [z.rim_width + i * z.cols for i in range(z.lines // STRIP)]
            last = [rim_ref[:STRIP, at : at + z.cols] for at in ats]
            total = total + jnp.concatenate(last, axis=0).astype(F32)
        total = total * (1.0 / dates_total)
        for d in range(z.dates):
            stage_q[d] = mean[d] * total
        q_copy = pltpu.make_async_copy(stage_q, quegan, sems.at[1])
        q_copy.start()
    assemble(z, tile, x_ref, rim_ref, 2 * low, 2 * (high - low))
    for first in range(0, high - low, GROUP):
        for d, _, mean, inv in look_stats(z, tile, first, min(GROUP, high - low - first), columns[...]):
            other_inv[d] = inv * (1.0 / LOOKS)
            other_log[d] = jnp.log(mean)
    take.wait()
    done = do_pairs(z, own, tile, z.dates + low, inv_ref, log_ref, other_inv, other_log, columns[...], lists, 2 + chunk, coh, logr, stage_coh, stage_log, sums, sems.at[0])
    done()
    if parts:
        q_copy.wait()


def vmem(n):
    return [pl.BlockSpec(memory_space=pltpu.VMEM)] * n


SMEM = pl.BlockSpec(memory_space=pltpu.SMEM)
HBM = pl.BlockSpec(memory_space=pltpu.HBM)
PARAMS = pltpu.CompilerParams(vmem_limit_bytes=50 * 1024 * 1024)
COST = pl.CostEstimate(flops=1, bytes_accessed=1, transcendentals=0)


def on_device(slc, lags):
    z = Sizes(slc, lags)
    shape = jax.ShapeDtypeStruct
    flat = slc.reshape(z.images * z.lines, z.cols)
    count = lax.axis_size("date")
    earlier = [(i, i - 1) for i in range(1, count)]
    later = [
        lax.ppermute(flat[2 * low * z.lines : 2 * high * z.lines], "date", earlier) for low, high in z.bounds
    ]
    packed = pl.pallas_call(
        lambda *refs: pack_kernel(z, *refs),
        out_shape=[shape((STRIP, HALF_AZ * z.cols), BF16)] * z.az
        + [shape((STRIP, z.images * z.lines + z.az * LANES), BF16)] * z.rng
        + [shape(flat.shape, BF16)],
        in_specs=vmem(1),
        out_specs=vmem(z.az + z.rng + 1),
        compiler_params=PARAMS,
        cost_estimate=COST,
        name="pack",
    )(flat)
    held = packed[z.az + z.rng]
    az, rng = sides("az", z.lines, HALF_AZ), sides("rng", z.cols, HALF_RG)

    lists_shape = (2 + CHUNKS, z.slot_count + 1)
    own_lists = pltpu.SMEM(lists_shape, jnp.int32)
    rim = [lax.ppermute(packed[i], "az", az[i][2]) for i in range(z.az)]
    lags, _ = lax.optimization_barrier((lags, rim[0]))
    columns, lists = pl.pallas_call(
        lambda *refs: prepare_kernel(z, *refs),
        out_shape=[shape((z.width, z.cols), BF16), shape(lists_shape, jnp.int32)],
        in_specs=[HBM],
        out_specs=vmem(2),
        scratch_shapes=[pltpu.SMEM(lags.shape, jnp.int32), own_lists, pltpu.SMEM((2 + CHUNKS,), jnp.int32)]
        + [pltpu.SemaphoreType.DMA],
        compiler_params=PARAMS,
        cost_estimate=COST,
        name="prepare",
    )(pltpu.with_memory_space_constraint(lags, pltpu.HBM))
    strips = [lax.ppermute(packed[z.az + j], "rng", rng[j][2]) for j in range(z.rng)]
    rim += [strip[:, : z.images * z.lines] for strip in strips]
    for i in range(z.az):
        for j in range(z.rng):
            strip, _ = lax.optimization_barrier((strips[j], columns))
            corner = lax.ppermute(strip, "az", az[i][2])
            rim.append(corner[:, z.images * z.lines + i * LANES :][:, :LANES])
    rim = jnp.concatenate(rim, axis=1)
    field = shape((z.dates, z.lines, z.cols), F32)
    out = shape((z.dates, z.slots, z.lines, z.cols), BF16)
    stage = pltpu.VMEM((z.slot_count, z.lines, z.cols), BF16)
    sums = pltpu.VMEM((2, 2 * GROUP * z.rows, z.cols), F32)
    sems = pltpu.SemaphoreType.DMA((2,))
    own, mean, inv, log, part, bundle = pl.pallas_call(
        lambda *refs: stats_kernel(z, *refs),
        out_shape=[shape((z.images, z.rows, z.width), BF16), field, field, field, shape((z.lines, z.cols), BF16)]
        + [shape((rim.shape[0], z.rim_width + z.cols * (z.lines // STRIP)), BF16)],
        in_specs=vmem(3),
        out_specs=vmem(6),
        compiler_params=PARAMS,
        cost_estimate=COST,
        name="stats",
    )(held, rim, columns)

    if 2 < count <= 4:
        later_rim = lax.ppermute(bundle, "date", [(i, (i - 1) % count) for i in range(count)])
        parts = [part]
        for k in range(2, count):
            parts.append(lax.ppermute(part, "date", [(i, (i - k) % count) for i in range(count)]))
    else:
        later_rim = lax.ppermute(rim, "date", earlier)
        parts = [lax.psum(part, "date")]

    coherence, log_ratio = pl.pallas_call(
        lambda *refs: own_kernel(z, *refs),
        out_shape=[out, out],
        in_specs=vmem(5),
        out_specs=[HBM] * 2,
        scratch_shapes=[stage, stage, sums, pltpu.VMEM((z.lines, z.cols), BF16), own_lists, sems],
        compiler_params=PARAMS,
        cost_estimate=COST,
        name="own",
    )(lists, columns, own, inv, log)

    for chunk, (low, high) in enumerate(z.bounds):
        last = chunk == len(z.bounds) - 1
        extra = [mean] + parts if last else []
        number = high - low
        other = pltpu.VMEM((number, z.lines, z.cols), F32)
        results = pl.pallas_call(
            lambda *refs, chunk=chunk, n=len(parts) if last else 0: cross_kernel(z, chunk, z.dates * count, n, *refs),
            out_shape=([field] if last else []) + [out, out],
            in_specs=vmem(7 + len(extra)) + [HBM] * 2,
            out_specs=([HBM] if last else []) + [HBM] * 2,
            scratch_shapes=[pltpu.VMEM((2 * number, z.rows, z.width), BF16), other, other, stage, stage, sums, own_lists, sems]
            + ([pltpu.VMEM(field.shape, F32)] if last else []),
            input_output_aliases={7 + len(extra): 1 if last else 0, 8 + len(extra): 2 if last else 1},
            compiler_params=PARAMS,
            cost_estimate=COST,
            name="cross",
        )(later[chunk], later_rim, lists, columns, own, inv, log, *extra, coherence, log_ratio)
        coherence, log_ratio = results[-2:]
    return coherence, log_ratio, results[0]


def solution(mesh):
    return jax.shard_map(
        on_device,
        mesh=mesh,
        in_specs=(P(("slab", "date"), None, "az", "rng"), P("date", None)),
        out_specs=(
            P(("slab", "date"), None, "az", "rng"),
            P(("slab", "date"), None, "az", "rng"),
            P(("slab", "date"), "az", "rng"),
        ),
        check_vma=False,
    )
```

```python
import jax
import jax.numpy as jnp
from jax import lax
from jax.experimental import pallas as pl
from jax.experimental.pallas import tpu as pltpu
from jax.sharding import PartitionSpec as P

HALF_AZ = 2
HALF_RG = 10
EPS = 1e-05
LOOKS = float((2 * HALF_AZ + 1) * (2 * HALF_RG + 1))

BF16 = jnp.bfloat16
F32 = jnp.float32
STRIP = 16
LANES = 128
GROUP = 4


def sides(axis, size, width):
    count = lax.axis_size(axis)
    me = lax.axis_index(axis)
    if count == 2:
        first = me == 0
        return [(jnp.where(first, size - width, 0), jnp.where(first, size, -width), [(0, 1), (1, 0)])]
    return [
        (size - width, -width, [(i, i + 1) for i in range(count - 1)]),
        (0, size, [(i + 1, i) for i in range(count - 1)]),
    ]


def marks(shape, where):
    row = lax.broadcasted_iota(jnp.int32, shape, 0)
    col = lax.broadcasted_iota(jnp.int32, shape, 1)
    return jnp.where(where(row, col), 1.0, 0.0).astype(BF16)


def dot(a, b, contract=(1, 0)):
    return lax.dot_general(a, b, (((contract[0],), (contract[1],)), ((), ())), preferred_element_type=F32)


class Sizes:
    def __init__(self, slc, lags):
        self.dates, _, self.lines, self.cols = slc.shape
        self.slots = lags.shape[1]
        self.images = 2 * self.dates
        self.az = 1 if lax.axis_size("az") == 2 else 2
        self.rng = 1 if lax.axis_size("rng") == 2 else 2
        self.rows = self.lines + STRIP
        self.width = self.cols + LANES
        self.slot_count = self.dates * self.slots
        self.rim_rows = 0
        self.rim_cols = self.az * HALF_AZ * self.cols
        self.rim_corners = self.rim_cols + self.rng * self.images * self.lines
        self.rim_width = self.rim_corners + self.az * self.rng * LANES


def make_lists(z, lags_ref, lists_ref, count_ref):
    for n in range(3):
        count_ref[n] = 0
    for d in range(z.dates):
        for s in range(z.slots):
            lag = lags_ref[d, s]
            which = jnp.where(lag > 0, jnp.where(d + lag < z.dates, 1, 2), 0)
            at = count_ref[which]
            lists_ref[which, at] = d * 65536 + s * 256 + d + lag
            count_ref[which] = at + 1
    for n in range(3):
        lists_ref[n, z.slot_count] = count_ref[n]


def places(z, axis, k, inside, tail, unit, width):
    at = jnp.where(k < inside, k, -(10**6))
    for j, (_, place, _) in enumerate(sides(axis, inside, width)):
        c = k - tail - j * unit
        at = jnp.where((c >= 0) & (c < width), place + c, at)
    return at


def near(a, b, reach):
    return jnp.where(jnp.abs(a - b) <= reach, 1.0, 0.0).astype(BF16)


def make_bands(z, columns_ref):
    at = places(z, "rng", lax.broadcasted_iota(jnp.int32, (z.width, 1), 0), z.cols, z.cols, STRIP, HALF_RG)
    columns_ref[...] = near(at, lax.broadcasted_iota(jnp.int32, (z.width, z.cols), 1), HALF_RG)


def pack_kernel(z, slc_ref, *out):
    held_ref, sem = out[z.az + z.rng + z.az * z.rng :]
    copy = pltpu.make_async_copy(slc_ref, held_ref, sem)
    copy.start()
    az, rng = sides("az", z.lines, HALF_AZ), sides("rng", z.cols, HALF_RG)
    picks = [marks((STRIP, z.cols), lambda c, k: (k == start + c) & (c < HALF_RG)) for start, _, _ in rng]
    copy.wait()
    x = held_ref[...]
    for i, (start, _, _) in enumerate(az):
        q = lax.broadcasted_iota(jnp.int32, (LANES, 1), 0)
        wanted = jnp.where(q < HALF_AZ * z.images, (q % z.images) * z.lines + start + q // z.images, -1)
        edge = dot(near(wanted, lax.broadcasted_iota(jnp.int32, (LANES, z.images * z.lines), 1), 0), x).astype(BF16)
        for r in range(HALF_AZ):
            out[i][:, r * z.cols : (r + 1) * z.cols] = edge[r * z.images : (r + 1) * z.images]
        for j, pick in enumerate(picks):
            out[z.az + z.rng + i * z.rng + j][...] = dot(pick, edge, (1, 1)).astype(BF16)
    for j, pick in enumerate(picks):
        out[z.az + j][...] = dot(pick, x, (1, 1)).astype(BF16)


def prepare_kernel(z, lags_ref, columns_ref, lists_ref, lags_s, lists_s, count_s, sem):
    take = pltpu.make_async_copy(lags_ref, lags_s, sem)
    take.start()
    make_bands(z, columns_ref)
    take.wait()
    make_lists(z, lags_s, lists_s, count_s)
    give = pltpu.make_async_copy(lists_s, lists_ref, sem)
    give.start()
    give.wait()


def assemble(z, tile_ref, x_ref, rim_ref, first, number):
    tile_ref[:, STRIP:, : z.cols] = x_ref[...].reshape(number, z.lines, z.cols)
    p = lax.broadcasted_iota(jnp.int32, (number * STRIP, 1), 0)
    az = [jnp.where(place < 0, STRIP + place, 0) for _, place, _ in sides("az", z.lines, HALF_AZ)]
    edge = jnp.zeros((number * STRIP, z.cols), F32)
    for i in range(z.az):
        for r in range(HALF_AZ):
            wanted = jnp.where(p % STRIP == az[i] + r, first + p // STRIP, -1)
            put = near(wanted, lax.broadcasted_iota(jnp.int32, (number * STRIP, z.images), 1), 0)
            at = (i * HALF_AZ + r) * z.cols
            edge = edge + dot(put, rim_ref[: z.images, at : at + z.cols])
    tile_ref[:, :STRIP, : z.cols] = edge.astype(BF16).reshape(number, STRIP, z.cols)
    side = jnp.zeros((number * z.lines, LANES), F32)
    corner = jnp.zeros((number * STRIP, LANES), F32)
    for j in range(z.rng):
        spread = marks((STRIP, LANES), lambda c, lane: lane == c + j * STRIP)
        at = z.rim_cols + (j * z.images + first) * z.lines
        side = side + dot(rim_ref[:STRIP, at : at + number * z.lines], spread, (0, 0))
        for i in range(z.az):
            at = z.rim_corners + (i * z.rng + j) * LANES
            turned = dot(rim_ref[:STRIP, at : at + LANES], spread, (0, 0)).astype(BF16)
            r = p % STRIP - az[i]
            wanted = jnp.where((r >= 0) & (r < HALF_AZ), r * z.images + first + p // STRIP, -1)
            put = near(wanted, lax.broadcasted_iota(jnp.int32, (number * STRIP, LANES), 1), 0)
            corner = corner + dot(put, turned)
    tile_ref[:, STRIP:, z.cols :] = side.astype(BF16).reshape(number, z.lines, LANES)
    tile_ref[:, :STRIP, z.cols :] = corner.astype(BF16).reshape(number, STRIP, LANES)


def split(x):
    high = x.astype(BF16)
    return high, (x - high.astype(F32)).astype(BF16)


def down_sums(z, x):
    half = STRIP // 2
    x = jnp.concatenate([x[half:], x[:half]], axis=0)
    top = half - HALF_AZ
    twos = x[top : top + z.lines + 3] + x[top + 1 : top + z.lines + 4]
    fours = twos[: z.lines + 1] + twos[2 : z.lines + 3]
    return fours[: z.lines] + x[half + HALF_AZ : half + HALF_AZ + z.lines]


def look_stats(z, tile, first, number, columns):
    powers, parts = [], []
    for d in range(first, first + number):
        re, im = tile[2 * d].astype(F32), tile[2 * d + 1].astype(F32)
        power = re * re + im * im
        powers.append(power[STRIP:, : z.cols])
        parts += split(power)
    sums = dot(jnp.concatenate(parts, axis=0), columns)
    for n, power in enumerate(powers):
        at = 2 * n * z.rows
        both = sums[at : at + z.rows] + sums[at + z.rows : at + 2 * z.rows]
        mean = down_sums(z, both) * (1.0 / LOOKS) + EPS
        yield first + n, power, mean, 1.0 / mean


def stats_kernel(z, x_ref, rim_ref, columns, tile_ref, mean_ref, inv_ref, log_ref, part_ref, bundle_ref):
    assemble(z, tile_ref, x_ref, rim_ref, 0, z.images)
    part = jnp.zeros((z.lines, z.cols), F32)
    for first in range(0, z.dates, GROUP):
        for d, power, mean, inv in look_stats(z, tile_ref, first, min(GROUP, z.dates - first), columns[...]):
            mean_ref[d] = mean
            inv_ref[d] = inv * (1.0 / LOOKS)
            log_ref[d] = jnp.log(mean)
            part = part + power * inv
    part = part.astype(BF16)
    part_ref[...] = part
    bundle_ref[:, : z.rim_width] = rim_ref[...]
    for i in range(z.lines // STRIP):
        at = z.rim_width + i * z.cols
        bundle_ref[:STRIP, at : at + z.cols] = part[i * STRIP : (i + 1) * STRIP]


def do_pairs(z, own, other, first_other, own_inv, own_log, other_inv, other_log, columns, lists, row, coh, log, emit=None):
    count = lists[row, z.slot_count]

    def pick(k):
        code = lists[row, jnp.minimum(k, count - 1)]
        return code // 65536, (code // 256) % 256, code % 256 - first_other

    def group(step, sent):
        picks = [pick(step * GROUP + g) for g in range(GROUP)]
        products = []
        for d, _, e in picks:
            a0, a1, b0, b1 = own[2 * d], own[2 * d + 1], other[2 * e], other[2 * e + 1]
            products += [a0 * b0 + a1 * b1, a1 * b0 - a0 * b1]
        sums = dot(jnp.concatenate(products, axis=0), columns)
        for g, (d, s, e) in enumerate(picks):
            at = 2 * g * z.rows
            re = down_sums(z, sums[at : at + z.rows])
            im = down_sums(z, sums[at + z.rows : at + 2 * z.rows])
            coh[d, s] = ((re * re + im * im) * (own_inv[d] * other_inv[e])).astype(BF16)
            log[d, s] = (own_log[d] - other_log[e]).astype(BF16)
        if emit is None:
            return sent
        following = (step + 1) * GROUP
        ready = jnp.where(following < count, pick(following)[0], z.dates)
        emit(sent, ready)
        return ready

    sent = lax.fori_loop(0, (count + GROUP - 1) // GROUP, group, 0)
    if emit is not None:
        emit(sent, z.dates)


def own_kernel(z, lists_ref, columns, tile, inv, log, coh, logr, lists, sem):
    take = pltpu.make_async_copy(lists_ref, lists, sem)
    take.start()
    take.wait()
    empty = jnp.zeros((z.lines, z.cols), BF16)

    def clear(k, _):
        code = lists[0, k]
        d, s = code // 65536, (code // 256) % 256
        coh[d, s] = empty
        logr[d, s] = empty
        return 0

    lax.fori_loop(0, lists[0, z.slot_count], clear, 0)
    do_pairs(z, tile, tile, 0, inv, log, inv, log, columns[...], lists, 1, coh, logr)


def cross_kernel(z, x_ref, rim_ref, lists_ref, columns, own, own_inv, own_log, coh_in, log_in, coh_out, log_out, tile, inv, log, lists, coh, logr, sems):
    takes = [
        pltpu.make_async_copy(lists_ref, lists, sems.at[0]),
        pltpu.make_async_copy(coh_in, coh, sems.at[1]),
        pltpu.make_async_copy(log_in, logr, sems.at[2]),
    ]
    for take in takes:
        take.start()
    assemble(z, tile, x_ref, rim_ref, 0, z.images)
    for first in range(0, z.dates, GROUP):
        for d, _, mean, inverse in look_stats(z, tile, first, min(GROUP, z.dates - first), columns[...]):
            inv[d] = inverse * (1.0 / LOOKS)
            log[d] = jnp.log(mean)
    for take in takes:
        take.wait()

    def copies(d):
        return (
            pltpu.make_async_copy(coh.at[d], coh_out.at[d], sems.at[3]),
            pltpu.make_async_copy(logr.at[d], log_out.at[d], sems.at[3]),
        )

    def emit(low, high):
        def start(d, _):
            for copy in copies(d):
                copy.start()
            return 0

        lax.fori_loop(low, high, start, 0)

    do_pairs(z, own, tile, z.dates, own_inv, own_log, inv, log, columns[...], lists, 2, coh, logr, emit)
    for d in range(z.dates):
        for copy in copies(d):
            copy.wait()


def quegan_kernel(z, dates_total, rotated, mean, rim_ref, *refs):
    parts, out = refs[:-1], refs[-1]
    total = parts[0][...].astype(F32)
    for part in parts[1:]:
        total = total + part[...].astype(F32)
    if rotated:
        ats = [z.rim_width + i * z.cols for i in range(z.lines // STRIP)]
        total = total + jnp.concatenate([rim_ref[:STRIP, at : at + z.cols] for at in ats], axis=0).astype(F32)
    total = total * (1.0 / dates_total)
    for d in range(z.dates):
        out[d] = mean[d] * total


def vmem(n):
    return [pl.BlockSpec(memory_space=pltpu.VMEM)] * n


SMEM = pl.BlockSpec(memory_space=pltpu.SMEM)
HBM = pl.BlockSpec(memory_space=pltpu.HBM)
PARAMS = pltpu.CompilerParams(vmem_limit_bytes=32 * 1024 * 1024)
COST = pl.CostEstimate(flops=1, bytes_accessed=1, transcendentals=0)


def on_device(slc, lags):
    z = Sizes(slc, lags)
    shape = jax.ShapeDtypeStruct
    flat = slc.reshape(z.images * z.lines, z.cols)
    count = lax.axis_size("date")
    earlier = [(i, i - 1) for i in range(1, count)]
    later = lax.ppermute(flat, "date", earlier)
    packed = pl.pallas_call(
        lambda *refs: pack_kernel(z, *refs),
        out_shape=[shape((STRIP, HALF_AZ * z.cols), BF16)] * z.az
        + [shape((STRIP, z.images * z.lines), BF16)] * z.rng
        + [shape((STRIP, LANES), BF16)] * (z.az * z.rng)
        + [shape(flat.shape, BF16)],
        in_specs=[HBM],
        out_specs=vmem(z.az + z.rng + z.az * z.rng + 1),
        scratch_shapes=[pltpu.SemaphoreType.DMA],
        compiler_params=PARAMS,
        cost_estimate=COST,
        name="pack",
    )(pltpu.with_memory_space_constraint(flat, pltpu.HBM))
    held = packed[-1]
    az, rng = sides("az", z.lines, HALF_AZ), sides("rng", z.cols, HALF_RG)

    lists_shape = (3, z.slot_count + 1)
    own_lists = pltpu.SMEM(lists_shape, jnp.int32)
    rim = [lax.ppermute(packed[i], "az", az[i][2]) for i in range(z.az)]
    lags, _ = lax.optimization_barrier((lags, packed[0]))
    columns, lists = pl.pallas_call(
        lambda *refs: prepare_kernel(z, *refs),
        out_shape=[shape((z.width, z.cols), BF16), shape(lists_shape, jnp.int32)],
        in_specs=[HBM],
        out_specs=vmem(2),
        scratch_shapes=[pltpu.SMEM(lags.shape, jnp.int32), own_lists, pltpu.SMEM((3,), jnp.int32)]
        + [pltpu.SemaphoreType.DMA],
        compiler_params=PARAMS,
        cost_estimate=COST,
        name="prepare",
    )(pltpu.with_memory_space_constraint(lags, pltpu.HBM))
    rim += [lax.ppermute(packed[z.az + j], "rng", rng[j][2]) for j in range(z.rng)]
    az_count = lax.axis_size("az")
    for i in range(z.az):
        for j in range(z.rng):
            pairs = [(a * az_count + b, c * az_count + d) for a, c in rng[j][2] for b, d in az[i][2]]
            rim.append(lax.ppermute(packed[z.az + z.rng + i * z.rng + j], ("rng", "az"), pairs))
    rim, _ = lax.optimization_barrier((rim, columns))
    rim = jnp.concatenate(rim, axis=1)
    field = shape((z.dates, z.lines, z.cols), F32)
    out = shape((z.dates, z.slots, z.lines, z.cols), BF16)
    own, mean, inv, log, part, bundle = pl.pallas_call(
        lambda *refs: stats_kernel(z, *refs),
        out_shape=[shape((z.images, z.rows, z.width), BF16), field, field, field, shape((z.lines, z.cols), BF16)]
        + [shape((rim.shape[0], z.rim_width + z.cols * (z.lines // STRIP)), BF16)],
        in_specs=vmem(3),
        out_specs=vmem(6),
        compiler_params=PARAMS,
        cost_estimate=COST,
        name="stats",
    )(held, rim, columns)

    rotated = 2 < count <= 4
    if rotated:
        later_rim = lax.ppermute(bundle, "date", [(i, (i - 1) % count) for i in range(count)])
        parts = [part]
        for k in range(2, count):
            parts.append(lax.ppermute(part, "date", [(i, (i - k) % count) for i in range(count)]))
    else:
        later_rim = lax.ppermute(rim, "date", earlier)
        parts = [lax.psum(part, "date")]

    coherence, log_ratio = pl.pallas_call(
        lambda *refs: own_kernel(z, *refs),
        out_shape=[out, out],
        in_specs=vmem(5),
        out_specs=vmem(2),
        scratch_shapes=[own_lists, pltpu.SemaphoreType.DMA],
        compiler_params=PARAMS,
        cost_estimate=COST,
        name="own",
    )(lists, columns, own, inv, log)
    other, held_out = pltpu.VMEM(field.shape, F32), pltpu.VMEM(out.shape, BF16)
    coherence, log_ratio = pl.pallas_call(
        lambda *refs: cross_kernel(z, *refs),
        out_shape=[out, out],
        in_specs=vmem(9),
        out_specs=[HBM] * 2,
        scratch_shapes=[pltpu.VMEM((z.images, z.rows, z.width), BF16), other, other, own_lists, held_out, held_out]
        + [pltpu.SemaphoreType.DMA((4,))],
        compiler_params=PARAMS,
        cost_estimate=COST,
        name="cross",
    )(later, later_rim, lists, columns, own, inv, log, coherence, log_ratio)
    mean, coherence, log_ratio = lax.optimization_barrier((mean, coherence, log_ratio))
    quegan = pl.pallas_call(
        lambda *refs: quegan_kernel(z, z.dates * count, rotated, *refs),
        out_shape=field,
        in_specs=vmem(2 + len(parts)),
        out_specs=vmem(1)[0],
        compiler_params=PARAMS,
        cost_estimate=COST,
        name="quegan",
    )(mean, later_rim, *parts)
    return coherence, log_ratio, quegan


def solution(mesh):
    return jax.shard_map(
        on_device,
        mesh=mesh,
        in_specs=(P(("slab", "date"), None, "az", "rng"), P("date", None)),
        out_specs=(
            P(("slab", "date"), None, "az", "rng"),
            P(("slab", "date"), None, "az", "rng"),
            P(("slab", "date"), "az", "rng"),
        ),
        check_vma=False,
    )
```

```python
import jax
import jax.numpy as jnp
from jax import lax
from jax.experimental import pallas as pl
from jax.experimental.pallas import tpu as pltpu
from jax.sharding import PartitionSpec as P

HALF_AZ = 2
HALF_RG = 10
EPS = 1e-05
LOOKS = float((2 * HALF_AZ + 1) * (2 * HALF_RG + 1))

BF16 = jnp.bfloat16
F32 = jnp.float32
STRIP = 16
LANES = 128
GROUP = 4
ENDS = (3, 5)
PARTS = 1


def sides(axis, size, width):
    count = lax.axis_size(axis)
    me = lax.axis_index(axis)
    if count == 2:
        first = me == 0
        return [(jnp.where(first, size - width, 0), jnp.where(first, size, -width), [(0, 1), (1, 0)])]
    return [
        (size - width, -width, [(i, i + 1) for i in range(count - 1)]),
        (0, size, [(i + 1, i) for i in range(count - 1)]),
    ]


def marks(shape, where):
    row = lax.broadcasted_iota(jnp.int32, shape, 0)
    col = lax.broadcasted_iota(jnp.int32, shape, 1)
    return jnp.where(where(row, col), 1.0, 0.0).astype(BF16)


def dot(a, b, contract=(1, 0)):
    return lax.dot_general(a, b, (((contract[0],), (contract[1],)), ((), ())), preferred_element_type=F32)


class Sizes:
    def __init__(self, slc, lags):
        self.dates, _, self.lines, self.cols = slc.shape
        self.slots = lags.shape[1]
        self.images = 2 * self.dates
        self.az = 1 if lax.axis_size("az") == 2 else 2
        self.rng = 1 if lax.axis_size("rng") == 2 else 2
        self.rows = self.lines + STRIP
        self.width = self.cols + LANES
        self.slot_count = self.dates * self.slots
        self.ends = tuple((self.dates * n) // 8 for n in ENDS)
        self.rim_rows = 0
        self.rim_cols = self.az * HALF_AZ * self.cols
        self.rim_corners = self.rim_cols + self.rng * self.images * self.lines
        self.rim_width = self.rim_corners + self.az * self.rng * LANES


def make_lists(z, lags_ref, lists_ref, count_ref):
    for n in range(3):
        count_ref[n] = 0
    for d in range(z.dates):
        for s in range(z.slots):
            lag = lags_ref[d, s]
            which = jnp.where(lag > 0, jnp.where(d + lag < z.dates, 1, 2), 0)
            at = count_ref[which]
            lists_ref[which, at] = d * 65536 + s * 256 + d + lag
            count_ref[which] = at + 1
    for n in range(3):
        lists_ref[n, z.slot_count] = count_ref[n]


def places(z, axis, k, inside, tail, unit, width):
    at = jnp.where(k < inside, k, -(10**6))
    for j, (_, place, _) in enumerate(sides(axis, inside, width)):
        c = k - tail - j * unit
        at = jnp.where((c >= 0) & (c < width), place + c, at)
    return at


def near(a, b, reach):
    return jnp.where(jnp.abs(a - b) <= reach, 1.0, 0.0).astype(BF16)


def make_bands(z, columns_ref):
    at = places(z, "rng", lax.broadcasted_iota(jnp.int32, (z.width, 1), 0), z.cols, z.cols, STRIP, HALF_RG)
    columns_ref[...] = near(at, lax.broadcasted_iota(jnp.int32, (z.width, z.cols), 1), HALF_RG)


def pack_kernel(z, slc_ref, *out):
    held_ref, sems = out[z.az + z.rng + z.az * z.rng :]
    part = z.images * z.lines // PARTS
    copies = [
        pltpu.make_async_copy(slc_ref.at[pl.ds(n * part, part)], held_ref.at[pl.ds(n * part, part)], sems.at[n])
        for n in range(PARTS)
    ]
    for copy in copies:
        copy.start()
    az, rng = sides("az", z.lines, HALF_AZ), sides("rng", z.cols, HALF_RG)
    picks, lanes = [], []
    for start, _, _ in rng:
        low = pl.multiple_of(jnp.where(start == 0, 0, z.cols - LANES), LANES)
        lanes.append(pl.ds(low, LANES))
        picks.append(marks((STRIP, LANES), lambda c, k: (k == start - low + c) & (c < HALF_RG)))
    for n, copy in enumerate(copies):
        copy.wait()
        for j, pick in enumerate(picks):
            columns = held_ref[n * part : (n + 1) * part, lanes[j]]
            out[z.az + j][:, n * part : (n + 1) * part] = dot(pick, columns, (1, 1)).astype(BF16)
    q = lax.broadcasted_iota(jnp.int32, (LANES, 1), 0)
    for i, (start, _, _) in enumerate(az):
        low = jnp.where(start == 0, 0, z.lines - STRIP)
        rows = [held_ref[pl.ds(pl.multiple_of(m * z.lines + low, STRIP), STRIP), :] for m in range(z.images)]
        wanted = jnp.where(q < HALF_AZ * z.images, (q % z.images) * STRIP + start - low + q // z.images, -1)
        put = near(wanted, lax.broadcasted_iota(jnp.int32, (LANES, z.images * STRIP), 1), 0)
        edge = dot(put, jnp.concatenate(rows, axis=0)).astype(BF16)
        for r in range(HALF_AZ):
            out[i][:, r * z.cols : (r + 1) * z.cols] = edge[r * z.images : (r + 1) * z.images]
        for j, (first, _, _) in enumerate(rng):
            pick = marks((STRIP, z.cols), lambda c, k: (k == first + c) & (c < HALF_RG))
            out[z.az + z.rng + i * z.rng + j][...] = dot(pick, edge, (1, 1)).astype(BF16)


def prepare_kernel(z, lags_ref, columns_ref, lists_ref, lags_s, lists_s, count_s, sem):
    take = pltpu.make_async_copy(lags_ref, lags_s, sem)
    take.start()
    make_bands(z, columns_ref)
    take.wait()
    make_lists(z, lags_s, lists_s, count_s)
    give = pltpu.make_async_copy(lists_s, lists_ref, sem)
    give.start()
    give.wait()


def assemble(z, tile_ref, x_ref, rim_ref, first, number):
    tile_ref[:, STRIP:, : z.cols] = x_ref[...].reshape(number, z.lines, z.cols)
    p = lax.broadcasted_iota(jnp.int32, (number * STRIP, 1), 0)
    az = [jnp.where(place < 0, STRIP + place, 0) for _, place, _ in sides("az", z.lines, HALF_AZ)]
    edge = jnp.zeros((number * STRIP, z.cols), F32)
    for i in range(z.az):
        for r in range(HALF_AZ):
            wanted = jnp.where(p % STRIP == az[i] + r, first + p // STRIP, -1)
            put = near(wanted, lax.broadcasted_iota(jnp.int32, (number * STRIP, z.images), 1), 0)
            at = (i * HALF_AZ + r) * z.cols
            edge = edge + dot(put, rim_ref[: z.images, at : at + z.cols])
    tile_ref[:, :STRIP, : z.cols] = edge.astype(BF16).reshape(number, STRIP, z.cols)
    side = jnp.zeros((number * z.lines, LANES), F32)
    corner = jnp.zeros((number * STRIP, LANES), F32)
    for j in range(z.rng):
        spread = marks((STRIP, LANES), lambda c, lane: lane == c + j * STRIP)
        at = z.rim_cols + (j * z.images + first) * z.lines
        side = side + dot(rim_ref[:STRIP, at : at + number * z.lines], spread, (0, 0))
        for i in range(z.az):
            at = z.rim_corners + (i * z.rng + j) * LANES
            turned = dot(rim_ref[:STRIP, at : at + LANES], spread, (0, 0)).astype(BF16)
            r = p % STRIP - az[i]
            wanted = jnp.where((r >= 0) & (r < HALF_AZ), r * z.images + first + p // STRIP, -1)
            put = near(wanted, lax.broadcasted_iota(jnp.int32, (number * STRIP, LANES), 1), 0)
            corner = corner + dot(put, turned)
    tile_ref[:, STRIP:, z.cols :] = side.astype(BF16).reshape(number, z.lines, LANES)
    tile_ref[:, :STRIP, z.cols :] = corner.astype(BF16).reshape(number, STRIP, LANES)


def split(x):
    high = x.astype(BF16)
    return high, (x - high.astype(F32)).astype(BF16)


def down_sums(z, x):
    half = STRIP // 2
    x = jnp.concatenate([x[half:], x[:half]], axis=0)
    top = half - HALF_AZ
    twos = x[top : top + z.lines + 3] + x[top + 1 : top + z.lines + 4]
    fours = twos[: z.lines + 1] + twos[2 : z.lines + 3]
    return fours[: z.lines] + x[half + HALF_AZ : half + HALF_AZ + z.lines]


def look_stats(z, tile, first, number, columns):
    powers, parts = [], []
    for d in range(first, first + number):
        re, im = tile[2 * d].astype(F32), tile[2 * d + 1].astype(F32)
        power = re * re + im * im
        powers.append(power[STRIP:, : z.cols])
        parts += split(power)
    sums = dot(jnp.concatenate(parts, axis=0), columns)
    for n, power in enumerate(powers):
        at = 2 * n * z.rows
        both = sums[at : at + z.rows] + sums[at + z.rows : at + 2 * z.rows]
        mean = down_sums(z, both) * (1.0 / LOOKS) + EPS
        yield first + n, power, mean, 1.0 / mean


def stats_kernel(z, x_ref, rim_ref, columns, tile_ref, mean_ref, inv_ref, log_ref, part_ref, bundle_ref):
    assemble(z, tile_ref, x_ref, rim_ref, 0, z.images)
    part = jnp.zeros((z.lines, z.cols), F32)
    for first in range(0, z.dates, GROUP):
        for d, power, mean, inv in look_stats(z, tile_ref, first, min(GROUP, z.dates - first), columns[...]):
            mean_ref[d] = mean
            inv_ref[d] = inv * (1.0 / LOOKS)
            log_ref[d] = jnp.log(mean)
            part = part + power * inv
    part = part.astype(BF16)
    part_ref[...] = part
    bundle_ref[:, : z.rim_width] = rim_ref[...]
    for i in range(z.lines // STRIP):
        at = z.rim_width + i * z.cols
        bundle_ref[:STRIP, at : at + z.cols] = part[i * STRIP : (i + 1) * STRIP]


def do_pairs(z, own, other, first_other, own_inv, own_log, other_inv, other_log, columns, lists, row, coh, log, emit=None):
    count = lists[row, z.slot_count]

    def pick(k):
        code = lists[row, jnp.minimum(k, count - 1)]
        return code // 65536, (code // 256) % 256, code % 256 - first_other

    def group(step, sent):
        picks = [pick(step * GROUP + g) for g in range(GROUP)]
        products = []
        for d, _, e in picks:
            a0, a1, b0, b1 = own[2 * d], own[2 * d + 1], other[2 * e], other[2 * e + 1]
            products += [a0 * b0 + a1 * b1, a1 * b0 - a0 * b1]
        sums = dot(jnp.concatenate(products, axis=0), columns)
        for g, (d, s, e) in enumerate(picks):
            at = 2 * g * z.rows
            re = down_sums(z, sums[at : at + z.rows])
            im = down_sums(z, sums[at + z.rows : at + 2 * z.rows])
            coh[d, s] = ((re * re + im * im) * (own_inv[d] * other_inv[e])).astype(BF16)
            log[d, s] = (own_log[d] - other_log[e]).astype(BF16)
        if emit is None:
            return sent
        following = (step + 1) * GROUP
        ready = jnp.where(following < count, pick(following)[0], z.dates)
        emit(sent, ready)
        return ready

    sent = lax.fori_loop(0, (count + GROUP - 1) // GROUP, group, 0)
    if emit is not None:
        emit(sent, z.dates)


def own_kernel(z, lists_ref, columns, tile, inv, log, coh, logr, lists, sem):
    take = pltpu.make_async_copy(lists_ref, lists, sem)
    take.start()
    take.wait()
    empty = jnp.zeros((z.lines, z.cols), BF16)

    def clear(k, _):
        code = lists[0, k]
        d, s = code // 65536, (code // 256) % 256
        coh[d, s] = empty
        logr[d, s] = empty
        return 0

    lax.fori_loop(0, lists[0, z.slot_count], clear, 0)
    do_pairs(z, tile, tile, 0, inv, log, inv, log, columns[...], lists, 1, coh, logr)


def cross_kernel(z, x_ref, rim_ref, lists_ref, columns, own, own_inv, own_log, coh_in, log_in, coh_out, log_out, coh_last, log_last, tile, inv, log, lists, coh, logr, sems):
    takes = [
        pltpu.make_async_copy(lists_ref, lists, sems.at[0]),
        pltpu.make_async_copy(coh_in, coh, sems.at[1]),
        pltpu.make_async_copy(log_in, logr, sems.at[2]),
    ]
    for take in takes:
        take.start()
    assemble(z, tile, x_ref, rim_ref, 0, z.images)
    for first in range(0, z.dates, GROUP):
        for d, _, mean, inverse in look_stats(z, tile, first, min(GROUP, z.dates - first), columns[...]):
            inv[d] = inverse * (1.0 / LOOKS)
            log[d] = jnp.log(mean)
    for take in takes:
        take.wait()

    spans = [(low, high - low) for low, high in zip((0,) + z.ends, z.ends)]

    def copies(low, number):
        span = pl.ds(low, number)
        return (
            pltpu.make_async_copy(coh.at[span], coh_out.at[span], sems.at[3]),
            pltpu.make_async_copy(logr.at[span], log_out.at[span], sems.at[3]),
        )

    def emit(sent, ready):
        for low, number in spans:

            @pl.when((sent < low + number) & (ready >= low + number))
            def _():
                for copy in copies(low, number):
                    copy.start()

    do_pairs(z, own, tile, z.dates, own_inv, own_log, inv, log, columns[...], lists, 2, coh, logr, emit)
    coh_last[...] = coh[z.ends[-1] :]
    log_last[...] = logr[z.ends[-1] :]
    for low, number in spans:
        for copy in copies(low, number):
            copy.wait()


def quegan_kernel(z, dates_total, rotated, coh_in, log_in, coh_last, log_last, mean, rim_ref, *refs):
    parts, (coh_out, log_out, out, stage, sems) = refs[:-5], refs[-5:]
    span = pl.ds(z.ends[-1], z.dates - z.ends[-1])
    copies = [
        pltpu.make_async_copy(coh_last, coh_out.at[span], sems.at[0]),
        pltpu.make_async_copy(log_last, log_out.at[span], sems.at[1]),
        pltpu.make_async_copy(stage, out, sems.at[2]),
    ]
    for copy in copies[:2]:
        copy.start()
    total = parts[0][...].astype(F32)
    for part in parts[1:]:
        total = total + part[...].astype(F32)
    if rotated:
        ats = [z.rim_width + i * z.cols for i in range(z.lines // STRIP)]
        total = total + jnp.concatenate([rim_ref[:STRIP, at : at + z.cols] for at in ats], axis=0).astype(F32)
    total = total * (1.0 / dates_total)
    for d in range(z.dates):
        stage[d] = mean[d] * total
    copies[2].start()
    for copy in copies:
        copy.wait()


def vmem(n):
    return [pl.BlockSpec(memory_space=pltpu.VMEM)] * n


SMEM = pl.BlockSpec(memory_space=pltpu.SMEM)
HBM = pl.BlockSpec(memory_space=pltpu.HBM)
PARAMS = pltpu.CompilerParams(vmem_limit_bytes=32 * 1024 * 1024)
COST = pl.CostEstimate(flops=1, bytes_accessed=1, transcendentals=0)


def on_device(slc, lags):
    z = Sizes(slc, lags)
    shape = jax.ShapeDtypeStruct
    flat = slc.reshape(z.images * z.lines, z.cols)
    count = lax.axis_size("date")
    earlier = [(i, i - 1) for i in range(1, count)]
    later = lax.ppermute(flat, "date", earlier)
    packed = pl.pallas_call(
        lambda *refs: pack_kernel(z, *refs),
        out_shape=[shape((STRIP, HALF_AZ * z.cols), BF16)] * z.az
        + [shape((STRIP, z.images * z.lines), BF16)] * z.rng
        + [shape((STRIP, LANES), BF16)] * (z.az * z.rng)
        + [shape(flat.shape, BF16)],
        in_specs=[HBM],
        out_specs=vmem(z.az + z.rng + z.az * z.rng + 1),
        scratch_shapes=[pltpu.SemaphoreType.DMA((PARTS,))],
        compiler_params=PARAMS,
        cost_estimate=COST,
        name="pack",
    )(pltpu.with_memory_space_constraint(flat, pltpu.HBM))
    held = packed[-1]
    az, rng = sides("az", z.lines, HALF_AZ), sides("rng", z.cols, HALF_RG)

    lists_shape = (3, z.slot_count + 1)
    own_lists = pltpu.SMEM(lists_shape, jnp.int32)
    rim = [lax.ppermute(packed[i], "az", az[i][2]) for i in range(z.az)]
    lags, _ = lax.optimization_barrier((lags, packed[0]))
    columns, lists = pl.pallas_call(
        lambda *refs: prepare_kernel(z, *refs),
        out_shape=[shape((z.width, z.cols), BF16), shape(lists_shape, jnp.int32)],
        in_specs=[HBM],
        out_specs=vmem(2),
        scratch_shapes=[pltpu.SMEM(lags.shape, jnp.int32), own_lists, pltpu.SMEM((3,), jnp.int32)]
        + [pltpu.SemaphoreType.DMA],
        compiler_params=PARAMS,
        cost_estimate=COST,
        name="prepare",
    )(pltpu.with_memory_space_constraint(lags, pltpu.HBM))
    rim += [lax.ppermute(packed[z.az + j], "rng", rng[j][2]) for j in range(z.rng)]
    az_count = lax.axis_size("az")
    for i in range(z.az):
        for j in range(z.rng):
            pairs = [(a * az_count + b, c * az_count + d) for a, c in rng[j][2] for b, d in az[i][2]]
            rim.append(lax.ppermute(packed[z.az + z.rng + i * z.rng + j], ("rng", "az"), pairs))
    rim, _ = lax.optimization_barrier((rim, columns))
    rim = jnp.concatenate(rim, axis=1)
    field = shape((z.dates, z.lines, z.cols), F32)
    out = shape((z.dates, z.slots, z.lines, z.cols), BF16)
    own, mean, inv, log, part, bundle = pl.pallas_call(
        lambda *refs: stats_kernel(z, *refs),
        out_shape=[shape((z.images, z.rows, z.width), BF16), field, field, field, shape((z.lines, z.cols), BF16)]
        + [shape((rim.shape[0], z.rim_width + z.cols * (z.lines // STRIP)), BF16)],
        in_specs=vmem(3),
        out_specs=vmem(6),
        compiler_params=PARAMS,
        cost_estimate=COST,
        name="stats",
    )(held, rim, columns)

    rotated = 2 < count <= 4
    if rotated:
        later_rim = lax.ppermute(bundle, "date", [(i, (i - 1) % count) for i in range(count)])
        parts = [part]
        for k in range(2, count):
            parts.append(lax.ppermute(part, "date", [(i, (i - k) % count) for i in range(count)]))
    else:
        later_rim = lax.ppermute(rim, "date", earlier)
        parts = [lax.psum(part, "date")]

    coherence, log_ratio = pl.pallas_call(
        lambda *refs: own_kernel(z, *refs),
        out_shape=[out, out],
        in_specs=vmem(5),
        out_specs=vmem(2),
        scratch_shapes=[own_lists, pltpu.SemaphoreType.DMA],
        compiler_params=PARAMS,
        cost_estimate=COST,
        name="own",
    )(lists, columns, own, inv, log)
    other, held_out = pltpu.VMEM(field.shape, F32), pltpu.VMEM(out.shape, BF16)
    last = shape((z.dates - z.ends[-1],) + out.shape[1:], BF16)
    coherence, log_ratio, coh_last, log_last = pl.pallas_call(
        lambda *refs: cross_kernel(z, *refs),
        out_shape=[out, out, last, last],
        in_specs=vmem(9),
        out_specs=[HBM] * 2 + vmem(2),
        scratch_shapes=[pltpu.VMEM((z.images, z.rows, z.width), BF16), other, other, own_lists, held_out, held_out]
        + [pltpu.SemaphoreType.DMA((4,))],
        compiler_params=PARAMS,
        cost_estimate=COST,
        name="cross",
    )(later, later_rim, lists, columns, own, inv, log, coherence, log_ratio)
    return pl.pallas_call(
        lambda *refs: quegan_kernel(z, z.dates * count, rotated, *refs),
        out_shape=(out, out, field),
        in_specs=[HBM] * 2 + vmem(4 + len(parts)),
        out_specs=(HBM, HBM, HBM),
        scratch_shapes=[pltpu.VMEM(field.shape, F32), pltpu.SemaphoreType.DMA((3,))],
        input_output_aliases={0: 0, 1: 1},
        compiler_params=PARAMS,
        cost_estimate=COST,
        name="quegan",
    )(coherence, log_ratio, coh_last, log_last, mean, later_rim, *parts)


def solution(mesh):
    return jax.shard_map(
        on_device,
        mesh=mesh,
        in_specs=(P(("slab", "date"), None, "az", "rng"), P("date", None)),
        out_specs=(
            P(("slab", "date"), None, "az", "rng"),
            P(("slab", "date"), None, "az", "rng"),
            P(("slab", "date"), "az", "rng"),
        ),
        check_vma=False,
    )
```

```python
import jax
import jax.numpy as jnp
from jax import lax
from jax.experimental import pallas as pl
from jax.experimental.pallas import tpu as pltpu
from jax.sharding import PartitionSpec as P

HALF_AZ = 2
HALF_RG = 10
EPS = 1e-05
LOOKS = float((2 * HALF_AZ + 1) * (2 * HALF_RG + 1))

BF16 = jnp.bfloat16
F32 = jnp.float32
STRIP = 16
LANES = 128
GROUP = 5
BATCH = 4
ENDS = (3, 5)
PARTS = 1


def sides(axis, size, width):
    count = lax.axis_size(axis)
    me = lax.axis_index(axis)
    if count == 2:
        first = me == 0
        return [(jnp.where(first, size - width, 0), jnp.where(first, size, -width), [(0, 1), (1, 0)])]
    return [
        (size - width, -width, [(i, i + 1) for i in range(count - 1)]),
        (0, size, [(i + 1, i) for i in range(count - 1)]),
    ]


def marks(shape, where):
    row = lax.broadcasted_iota(jnp.int32, shape, 0)
    col = lax.broadcasted_iota(jnp.int32, shape, 1)
    return jnp.where(where(row, col), 1.0, 0.0).astype(BF16)


def dot(a, b, contract=(1, 0)):
    return lax.dot_general(a, b, (((contract[0],), (contract[1],)), ((), ())), preferred_element_type=F32)


class Sizes:
    def __init__(self, slc, lags):
        self.dates, _, self.lines, self.cols = slc.shape
        self.slots = lags.shape[1]
        self.images = 2 * self.dates
        self.az = 1 if lax.axis_size("az") == 2 else 2
        self.rng = 1 if lax.axis_size("rng") == 2 else 2
        self.rows = self.lines + STRIP
        self.width = self.cols + LANES
        self.slot_count = self.dates * self.slots
        self.ends = tuple((self.dates * n) // 8 for n in ENDS)
        self.rim_rows = 0
        self.rim_cols = self.az * HALF_AZ * self.cols
        self.rim_corners = self.rim_cols + self.rng * self.images * self.lines
        self.rim_width = self.rim_corners + self.az * self.rng * LANES


def make_lists(z, lags_ref, lists_ref, count_ref):
    for n in range(3):
        count_ref[n] = 0
    for d in range(z.dates):
        for s in range(z.slots):
            lag = lags_ref[d, s]
            which = jnp.where(lag > 0, jnp.where(d + lag < z.dates, 1, 2), 0)
            at = count_ref[which]
            lists_ref[which, at] = d * 65536 + s * 256 + d + lag
            count_ref[which] = at + 1
    for n in range(3):
        lists_ref[n, z.slot_count] = count_ref[n]


def places(z, axis, k, inside, tail, unit, width):
    at = jnp.where(k < inside, k, -(10**6))
    for j, (_, place, _) in enumerate(sides(axis, inside, width)):
        c = k - tail - j * unit
        at = jnp.where((c >= 0) & (c < width), place + c, at)
    return at


def near(a, b, reach):
    return jnp.where(jnp.abs(a - b) <= reach, 1.0, 0.0).astype(BF16)


def make_bands(z, columns_ref):
    at = places(z, "rng", lax.broadcasted_iota(jnp.int32, (z.width, 1), 0), z.cols, z.cols, STRIP, HALF_RG)
    columns_ref[...] = near(at, lax.broadcasted_iota(jnp.int32, (z.width, z.cols), 1), HALF_RG)


def pack_kernel(z, slc_ref, *out):
    held_ref, sems = out[z.az + z.rng + z.az * z.rng :]
    part = z.images * z.lines // PARTS
    copies = [
        pltpu.make_async_copy(slc_ref.at[pl.ds(n * part, part)], held_ref.at[pl.ds(n * part, part)], sems.at[n])
        for n in range(PARTS)
    ]
    for copy in copies:
        copy.start()
    az, rng = sides("az", z.lines, HALF_AZ), sides("rng", z.cols, HALF_RG)
    picks, lanes = [], []
    for start, _, _ in rng:
        low = pl.multiple_of(jnp.where(start == 0, 0, z.cols - LANES), LANES)
        lanes.append(pl.ds(low, LANES))
        picks.append(marks((STRIP, LANES), lambda c, k: (k == start - low + c) & (c < HALF_RG)))
    for n, copy in enumerate(copies):
        copy.wait()
        for j, pick in enumerate(picks):
            columns = held_ref[n * part : (n + 1) * part, lanes[j]]
            out[z.az + j][:, n * part : (n + 1) * part] = dot(pick, columns, (1, 1)).astype(BF16)
    q = lax.broadcasted_iota(jnp.int32, (LANES, 1), 0)
    for i, (start, _, _) in enumerate(az):
        low = jnp.where(start == 0, 0, z.lines - STRIP)
        rows = [held_ref[pl.ds(pl.multiple_of(m * z.lines + low, STRIP), STRIP), :] for m in range(z.images)]
        wanted = jnp.where(q < HALF_AZ * z.images, (q % z.images) * STRIP + start - low + q // z.images, -1)
        put = near(wanted, lax.broadcasted_iota(jnp.int32, (LANES, z.images * STRIP), 1), 0)
        edge = dot(put, jnp.concatenate(rows, axis=0)).astype(BF16)
        for r in range(HALF_AZ):
            out[i][:, r * z.cols : (r + 1) * z.cols] = edge[r * z.images : (r + 1) * z.images]
        for j, (first, _, _) in enumerate(rng):
            pick = marks((STRIP, z.cols), lambda c, k: (k == first + c) & (c < HALF_RG))
            out[z.az + z.rng + i * z.rng + j][...] = dot(pick, edge, (1, 1)).astype(BF16)


def prepare_kernel(z, lags_ref, columns_ref, lists_ref, lags_s, lists_s, count_s, sem):
    take = pltpu.make_async_copy(lags_ref, lags_s, sem)
    take.start()
    make_bands(z, columns_ref)
    take.wait()
    make_lists(z, lags_s, lists_s, count_s)
    give = pltpu.make_async_copy(lists_s, lists_ref, sem)
    give.start()
    give.wait()


def assemble(z, tile_ref, x_ref, rim_ref, first, number):
    tile_ref[:, STRIP:, : z.cols] = x_ref[...].reshape(number, z.lines, z.cols)
    p = lax.broadcasted_iota(jnp.int32, (number * STRIP, 1), 0)
    az = [jnp.where(place < 0, STRIP + place, 0) for _, place, _ in sides("az", z.lines, HALF_AZ)]
    edge = jnp.zeros((number * STRIP, z.cols), F32)
    for i in range(z.az):
        for r in range(HALF_AZ):
            wanted = jnp.where(p % STRIP == az[i] + r, first + p // STRIP, -1)
            put = near(wanted, lax.broadcasted_iota(jnp.int32, (number * STRIP, z.images), 1), 0)
            at = (i * HALF_AZ + r) * z.cols
            edge = edge + dot(put, rim_ref[: z.images, at : at + z.cols])
    tile_ref[:, :STRIP, : z.cols] = edge.astype(BF16).reshape(number, STRIP, z.cols)
    side = jnp.zeros((number * z.lines, LANES), F32)
    corner = jnp.zeros((number * STRIP, LANES), F32)
    for j in range(z.rng):
        spread = marks((STRIP, LANES), lambda c, lane: lane == c + j * STRIP)
        at = z.rim_cols + (j * z.images + first) * z.lines
        side = side + dot(rim_ref[:STRIP, at : at + number * z.lines], spread, (0, 0))
        for i in range(z.az):
            at = z.rim_corners + (i * z.rng + j) * LANES
            turned = dot(rim_ref[:STRIP, at : at + LANES], spread, (0, 0)).astype(BF16)
            r = p % STRIP - az[i]
            wanted = jnp.where((r >= 0) & (r < HALF_AZ), r * z.images + first + p // STRIP, -1)
            put = near(wanted, lax.broadcasted_iota(jnp.int32, (number * STRIP, LANES), 1), 0)
            corner = corner + dot(put, turned)
    tile_ref[:, STRIP:, z.cols :] = side.astype(BF16).reshape(number, z.lines, LANES)
    tile_ref[:, :STRIP, z.cols :] = corner.astype(BF16).reshape(number, STRIP, LANES)


def split(x):
    high = x.astype(BF16)
    return high, (x - high.astype(F32)).astype(BF16)


def down_sums(z, x):
    half = STRIP // 2
    x = jnp.concatenate([x[half:], x[:half]], axis=0)
    top = half - HALF_AZ
    twos = x[top : top + z.lines + 3] + x[top + 1 : top + z.lines + 4]
    fours = twos[: z.lines + 1] + twos[2 : z.lines + 3]
    return fours[: z.lines] + x[half + HALF_AZ : half + HALF_AZ + z.lines]


def look_stats(z, tile, first, number, columns):
    powers, parts = [], []
    for d in range(first, first + number):
        re, im = tile[2 * d].astype(F32), tile[2 * d + 1].astype(F32)
        power = re * re + im * im
        powers.append(power[STRIP:, : z.cols])
        parts += split(power)
    sums = dot(jnp.concatenate(parts, axis=0), columns)
    for n, power in enumerate(powers):
        at = 2 * n * z.rows
        both = sums[at : at + z.rows] + sums[at + z.rows : at + 2 * z.rows]
        mean = down_sums(z, both) * (1.0 / LOOKS) + EPS
        yield first + n, power, mean, 1.0 / mean


def stats_kernel(z, x_ref, rim_ref, columns, tile_ref, mean_ref, inv_ref, log_ref, part_ref, bundle_ref):
    assemble(z, tile_ref, x_ref, rim_ref, 0, z.images)
    part = jnp.zeros((z.lines, z.cols), F32)
    for first in range(0, z.dates, BATCH):
        for d, power, mean, inv in look_stats(z, tile_ref, first, min(BATCH, z.dates - first), columns[...]):
            mean_ref[d] = mean
            inv_ref[d] = inv * (1.0 / LOOKS)
            log_ref[d] = jnp.log(mean)
            part = part + power * inv
    part = part.astype(BF16)
    part_ref[...] = part
    bundle_ref[:, : z.rim_width] = rim_ref[...]
    for i in range(z.lines // STRIP):
        at = z.rim_width + i * z.cols
        bundle_ref[:STRIP, at : at + z.cols] = part[i * STRIP : (i + 1) * STRIP]


def do_pairs(z, own, other, first_other, own_inv, own_log, other_inv, other_log, columns, lists, row, coh, log, emit=None):
    count = lists[row, z.slot_count]

    def pick(k):
        code = lists[row, jnp.minimum(k, count - 1)]
        return code // 65536, (code // 256) % 256, code % 256 - first_other

    def group(step, sent):
        picks = [pick(step * GROUP + g) for g in range(GROUP)]
        products = []
        for d, _, e in picks:
            a0, a1, b0, b1 = own[2 * d], own[2 * d + 1], other[2 * e], other[2 * e + 1]
            products += [a0 * b0 + a1 * b1, a1 * b0 - a0 * b1]
        sums = dot(jnp.concatenate(products, axis=0), columns)
        for g, (d, s, e) in enumerate(picks):
            at = 2 * g * z.rows
            re = down_sums(z, sums[at : at + z.rows])
            im = down_sums(z, sums[at + z.rows : at + 2 * z.rows])
            coh[d, s] = ((re * re + im * im) * (own_inv[d] * other_inv[e])).astype(BF16)
            log[d, s] = (own_log[d] - other_log[e]).astype(BF16)
        if emit is None:
            return sent
        following = (step + 1) * GROUP
        ready = jnp.where(following < count, pick(following)[0], z.dates)
        emit(sent, ready)
        return ready

    sent = lax.fori_loop(0, (count + GROUP - 1) // GROUP, group, 0)
    if emit is not None:
        emit(sent, z.dates)


def own_kernel(z, lists_ref, columns, tile, inv, log, coh, logr, lists, sem):
    take = pltpu.make_async_copy(lists_ref, lists, sem)
    take.start()
    take.wait()
    empty = jnp.zeros((z.lines, z.cols), BF16)

    def clear(k, _):
        code = lists[0, k]
        d, s = code // 65536, (code // 256) % 256
        coh[d, s] = empty
        logr[d, s] = empty
        return 0

    lax.fori_loop(0, lists[0, z.slot_count], clear, 0)
    do_pairs(z, tile, tile, 0, inv, log, inv, log, columns[...], lists, 1, coh, logr)


def cross_kernel(z, x_ref, rim_ref, lists_ref, columns, own, own_inv, own_log, coh_in, log_in, coh_out, log_out, coh_last, log_last, tile, inv, log, lists, coh, logr, sems):
    takes = [
        pltpu.make_async_copy(lists_ref, lists, sems.at[0]),
        pltpu.make_async_copy(coh_in, coh, sems.at[1]),
        pltpu.make_async_copy(log_in, logr, sems.at[2]),
    ]
    for take in takes:
        take.start()
    assemble(z, tile, x_ref, rim_ref, 0, z.images)
    for first in range(0, z.dates, BATCH):
        for d, _, mean, inverse in look_stats(z, tile, first, min(BATCH, z.dates - first), columns[...]):
            inv[d] = inverse * (1.0 / LOOKS)
            log[d] = jnp.log(mean)
    for take in takes:
        take.wait()

    spans = [(low, high - low) for low, high in zip((0,) + z.ends, z.ends)]

    def copies(low, number):
        span = pl.ds(low, number)
        return (
            pltpu.make_async_copy(coh.at[span], coh_out.at[span], sems.at[3]),
            pltpu.make_async_copy(logr.at[span], log_out.at[span], sems.at[3]),
        )

    def emit(sent, ready):
        for low, number in spans:

            @pl.when((sent < low + number) & (ready >= low + number))
            def _():
                for copy in copies(low, number):
                    copy.start()

    do_pairs(z, own, tile, z.dates, own_inv, own_log, inv, log, columns[...], lists, 2, coh, logr, emit)
    coh_last[...] = coh[z.ends[-1] :]
    log_last[...] = logr[z.ends[-1] :]
    for low, number in spans:
        for copy in copies(low, number):
            copy.wait()


def quegan_kernel(z, dates_total, rotated, coh_in, log_in, coh_last, log_last, mean, rim_ref, *refs):
    parts, (coh_out, log_out, out, stage, sems) = refs[:-5], refs[-5:]
    span = pl.ds(z.ends[-1], z.dates - z.ends[-1])
    copies = [
        pltpu.make_async_copy(coh_last, coh_out.at[span], sems.at[0]),
        pltpu.make_async_copy(log_last, log_out.at[span], sems.at[1]),
        pltpu.make_async_copy(stage, out, sems.at[2]),
    ]
    for copy in copies[:2]:
        copy.start()
    total = parts[0][...].astype(F32)
    for part in parts[1:]:
        total = total + part[...].astype(F32)
    if rotated:
        ats = [z.rim_width + i * z.cols for i in range(z.lines // STRIP)]
        total = total + jnp.concatenate([rim_ref[:STRIP, at : at + z.cols] for at in ats], axis=0).astype(F32)
    total = total * (1.0 / dates_total)
    for d in range(z.dates):
        stage[d] = mean[d] * total
    copies[2].start()
    for copy in copies:
        copy.wait()


def vmem(n):
    return [pl.BlockSpec(memory_space=pltpu.VMEM)] * n


SMEM = pl.BlockSpec(memory_space=pltpu.SMEM)
HBM = pl.BlockSpec(memory_space=pltpu.HBM)
PARAMS = pltpu.CompilerParams(vmem_limit_bytes=32 * 1024 * 1024)
COST = pl.CostEstimate(flops=1, bytes_accessed=1, transcendentals=0)


def on_device(slc, lags):
    z = Sizes(slc, lags)
    shape = jax.ShapeDtypeStruct
    flat = slc.reshape(z.images * z.lines, z.cols)
    count = lax.axis_size("date")
    earlier = [(i, i - 1) for i in range(1, count)]
    later = lax.ppermute(flat, "date", earlier)
    packed = pl.pallas_call(
        lambda *refs: pack_kernel(z, *refs),
        out_shape=[shape((STRIP, HALF_AZ * z.cols), BF16)] * z.az
        + [shape((STRIP, z.images * z.lines), BF16)] * z.rng
        + [shape((STRIP, LANES), BF16)] * (z.az * z.rng)
        + [shape(flat.shape, BF16)],
        in_specs=[HBM],
        out_specs=vmem(z.az + z.rng + z.az * z.rng + 1),
        scratch_shapes=[pltpu.SemaphoreType.DMA((PARTS,))],
        compiler_params=PARAMS,
        cost_estimate=COST,
        name="pack",
    )(pltpu.with_memory_space_constraint(flat, pltpu.HBM))
    held = packed[-1]
    az, rng = sides("az", z.lines, HALF_AZ), sides("rng", z.cols, HALF_RG)

    lists_shape = (3, z.slot_count + 1)
    own_lists = pltpu.SMEM(lists_shape, jnp.int32)
    rim = [lax.ppermute(packed[i], "az", az[i][2]) for i in range(z.az)]
    lags, _ = lax.optimization_barrier((lags, packed[0]))
    columns, lists = pl.pallas_call(
        lambda *refs: prepare_kernel(z, *refs),
        out_shape=[shape((z.width, z.cols), BF16), shape(lists_shape, jnp.int32)],
        in_specs=[HBM],
        out_specs=vmem(2),
        scratch_shapes=[pltpu.SMEM(lags.shape, jnp.int32), own_lists, pltpu.SMEM((3,), jnp.int32)]
        + [pltpu.SemaphoreType.DMA],
        compiler_params=PARAMS,
        cost_estimate=COST,
        name="prepare",
    )(pltpu.with_memory_space_constraint(lags, pltpu.HBM))
    rim += [lax.ppermute(packed[z.az + j], "rng", rng[j][2]) for j in range(z.rng)]
    az_count = lax.axis_size("az")
    for i in range(z.az):
        for j in range(z.rng):
            pairs = [(a * az_count + b, c * az_count + d) for a, c in rng[j][2] for b, d in az[i][2]]
            rim.append(lax.ppermute(packed[z.az + z.rng + i * z.rng + j], ("rng", "az"), pairs))
    rim, _ = lax.optimization_barrier((rim, columns))
    rim = jnp.concatenate(rim, axis=1)
    field = shape((z.dates, z.lines, z.cols), F32)
    out = shape((z.dates, z.slots, z.lines, z.cols), BF16)
    own, mean, inv, log, part, bundle = pl.pallas_call(
        lambda *refs: stats_kernel(z, *refs),
        out_shape=[shape((z.images, z.rows, z.width), BF16), field, field, field, shape((z.lines, z.cols), BF16)]
        + [shape((rim.shape[0], z.rim_width + z.cols * (z.lines // STRIP)), BF16)],
        in_specs=vmem(3),
        out_specs=vmem(6),
        compiler_params=PARAMS,
        cost_estimate=COST,
        name="stats",
    )(held, rim, columns)

    rotated = 2 < count <= 4
    if rotated:
        later_rim = lax.ppermute(bundle, "date", [(i, (i - 1) % count) for i in range(count)])
        parts = [part]
        for k in range(2, count):
            parts.append(lax.ppermute(part, "date", [(i, (i - k) % count) for i in range(count)]))
    else:
        later_rim = lax.ppermute(rim, "date", earlier)
        parts = [lax.psum(part, "date")]

    coherence, log_ratio = pl.pallas_call(
        lambda *refs: own_kernel(z, *refs),
        out_shape=[out, out],
        in_specs=vmem(5),
        out_specs=vmem(2),
        scratch_shapes=[own_lists, pltpu.SemaphoreType.DMA],
        compiler_params=PARAMS,
        cost_estimate=COST,
        name="own",
    )(lists, columns, own, inv, log)
    other, held_out = pltpu.VMEM(field.shape, F32), pltpu.VMEM(out.shape, BF16)
    last = shape((z.dates - z.ends[-1],) + out.shape[1:], BF16)
    coherence, log_ratio, coh_last, log_last = pl.pallas_call(
        lambda *refs: cross_kernel(z, *refs),
        out_shape=[out, out, last, last],
        in_specs=vmem(9),
        out_specs=[HBM] * 2 + vmem(2),
        scratch_shapes=[pltpu.VMEM((z.images, z.rows, z.width), BF16), other, other, own_lists, held_out, held_out]
        + [pltpu.SemaphoreType.DMA((4,))],
        compiler_params=PARAMS,
        cost_estimate=COST,
        name="cross",
    )(later, later_rim, lists, columns, own, inv, log, coherence, log_ratio)
    return pl.pallas_call(
        lambda *refs: quegan_kernel(z, z.dates * count, rotated, *refs),
        out_shape=(out, out, field),
        in_specs=[HBM] * 2 + vmem(4 + len(parts)),
        out_specs=(HBM, HBM, HBM),
        scratch_shapes=[pltpu.VMEM(field.shape, F32), pltpu.SemaphoreType.DMA((3,))],
        input_output_aliases={0: 0, 1: 1},
        compiler_params=PARAMS,
        cost_estimate=COST,
        name="quegan",
    )(coherence, log_ratio, coh_last, log_last, mean, later_rim, *parts)


def solution(mesh):
    return jax.shard_map(
        on_device,
        mesh=mesh,
        in_specs=(P(("slab", "date"), None, "az", "rng"), P("date", None)),
        out_specs=(
            P(("slab", "date"), None, "az", "rng"),
            P(("slab", "date"), None, "az", "rng"),
            P(("slab", "date"), "az", "rng"),
        ),
        check_vma=False,
    )
```

```python
import jax
import jax.numpy as jnp
from jax import lax
from jax.experimental import pallas as pl
from jax.experimental.pallas import tpu as pltpu
from jax.sharding import PartitionSpec as P

HALF_AZ = 2
HALF_RG = 10
EPS = 1e-05
LOOKS = float((2 * HALF_AZ + 1) * (2 * HALF_RG + 1))

BF16 = jnp.bfloat16
F32 = jnp.float32
STRIP = 16
LANES = 128
GROUP = 5
BATCH = 4
ENDS = (3, 5)
PARTS = 1


def sides(axis, size, width):
    count = lax.axis_size(axis)
    me = lax.axis_index(axis)
    if count == 2:
        first = me == 0
        return [(jnp.where(first, size - width, 0), jnp.where(first, size, -width), [(0, 1), (1, 0)])]
    return [
        (size - width, -width, [(i, i + 1) for i in range(count - 1)]),
        (0, size, [(i + 1, i) for i in range(count - 1)]),
    ]


def marks(shape, where):
    row = lax.broadcasted_iota(jnp.int32, shape, 0)
    col = lax.broadcasted_iota(jnp.int32, shape, 1)
    return jnp.where(where(row, col), 1.0, 0.0).astype(BF16)


def dot(a, b, contract=(1, 0)):
    return lax.dot_general(a, b, (((contract[0],), (contract[1],)), ((), ())), preferred_element_type=F32)


class Sizes:
    def __init__(self, slc, lags):
        self.dates, _, self.lines, self.cols = slc.shape
        self.slots = lags.shape[1]
        self.images = 2 * self.dates
        self.az = 1 if lax.axis_size("az") == 2 else 2
        self.rng = 1 if lax.axis_size("rng") == 2 else 2
        self.rows = self.lines + STRIP
        self.width = self.cols + LANES
        self.slot_count = self.dates * self.slots
        self.ends = tuple((self.dates * n) // 8 for n in ENDS)
        self.rim_rows = 0
        self.rim_cols = self.az * HALF_AZ * self.cols
        self.rim_corners = self.rim_cols + self.rng * self.images * self.lines
        self.rim_width = self.rim_corners + self.az * self.rng * LANES


def make_lists(z, lags_ref, lists_ref, count_ref):
    for n in range(3):
        count_ref[n] = 0
    for d in range(z.dates):
        for s in range(z.slots):
            lag = lags_ref[d, s]
            which = jnp.where(lag > 0, jnp.where(d + lag < z.dates, 1, 2), 0)
            at = count_ref[which]
            lists_ref[which, at] = d * 65536 + s * 256 + d + lag
            count_ref[which] = at + 1
    for n in range(3):
        lists_ref[n, z.slot_count] = count_ref[n]


def places(z, axis, k, inside, tail, unit, width):
    at = jnp.where(k < inside, k, -(10**6))
    for j, (_, place, _) in enumerate(sides(axis, inside, width)):
        c = k - tail - j * unit
        at = jnp.where((c >= 0) & (c < width), place + c, at)
    return at


def near(a, b, reach):
    return jnp.where(jnp.abs(a - b) <= reach, 1.0, 0.0).astype(BF16)


def make_bands(z, columns_ref):
    at = places(z, "rng", lax.broadcasted_iota(jnp.int32, (z.width, 1), 0), z.cols, z.cols, STRIP, HALF_RG)
    columns_ref[...] = near(at, lax.broadcasted_iota(jnp.int32, (z.width, z.cols), 1), HALF_RG)


def pack_kernel(z, slc_ref, *out):
    held_ref, sems = out[z.az + z.rng + z.az * z.rng :]
    part = z.images * z.lines // PARTS
    copies = [
        pltpu.make_async_copy(slc_ref.at[pl.ds(n * part, part)], held_ref.at[pl.ds(n * part, part)], sems.at[n])
        for n in range(PARTS)
    ]
    for copy in copies:
        copy.start()
    az, rng = sides("az", z.lines, HALF_AZ), sides("rng", z.cols, HALF_RG)
    picks, lanes = [], []
    for start, _, _ in rng:
        low = pl.multiple_of(jnp.where(start == 0, 0, z.cols - LANES), LANES)
        lanes.append(pl.ds(low, LANES))
        picks.append(marks((STRIP, LANES), lambda c, k: (k == start - low + c) & (c < HALF_RG)))
    for n, copy in enumerate(copies):
        copy.wait()
        for j, pick in enumerate(picks):
            columns = held_ref[n * part : (n + 1) * part, lanes[j]]
            out[z.az + j][:, n * part : (n + 1) * part] = dot(pick, columns, (1, 1)).astype(BF16)
    q = lax.broadcasted_iota(jnp.int32, (LANES, 1), 0)
    for i, (start, _, _) in enumerate(az):
        low = jnp.where(start == 0, 0, z.lines - STRIP)
        rows = [held_ref[pl.ds(pl.multiple_of(m * z.lines + low, STRIP), STRIP), :] for m in range(z.images)]
        wanted = jnp.where(q < HALF_AZ * z.images, (q % z.images) * STRIP + start - low + q // z.images, -1)
        put = near(wanted, lax.broadcasted_iota(jnp.int32, (LANES, z.images * STRIP), 1), 0)
        edge = dot(put, jnp.concatenate(rows, axis=0)).astype(BF16)
        for r in range(HALF_AZ):
            out[i][:, r * z.cols : (r + 1) * z.cols] = edge[r * z.images : (r + 1) * z.images]
        for j, (first, _, _) in enumerate(rng):
            pick = marks((STRIP, z.cols), lambda c, k: (k == first + c) & (c < HALF_RG))
            out[z.az + z.rng + i * z.rng + j][...] = dot(pick, edge, (1, 1)).astype(BF16)


def prepare_kernel(z, lags_ref, columns_ref, lists_ref, lags_s, lists_s, count_s, sem):
    take = pltpu.make_async_copy(lags_ref, lags_s, sem)
    take.start()
    make_bands(z, columns_ref)
    take.wait()
    make_lists(z, lags_s, lists_s, count_s)
    give = pltpu.make_async_copy(lists_s, lists_ref, sem)
    give.start()
    give.wait()


def assemble(z, tile_ref, x_ref, rim_ref, first, number):
    tile_ref[:, STRIP:, : z.cols] = x_ref[...].reshape(number, z.lines, z.cols)
    p = lax.broadcasted_iota(jnp.int32, (number * STRIP, 1), 0)
    az = [jnp.where(place < 0, STRIP + place, 0) for _, place, _ in sides("az", z.lines, HALF_AZ)]
    edge = jnp.zeros((number * STRIP, z.cols), F32)
    for i in range(z.az):
        for r in range(HALF_AZ):
            wanted = jnp.where(p % STRIP == az[i] + r, first + p // STRIP, -1)
            put = near(wanted, lax.broadcasted_iota(jnp.int32, (number * STRIP, z.images), 1), 0)
            at = (i * HALF_AZ + r) * z.cols
            edge = edge + dot(put, rim_ref[: z.images, at : at + z.cols])
    tile_ref[:, :STRIP, : z.cols] = edge.astype(BF16).reshape(number, STRIP, z.cols)
    side = jnp.zeros((number * z.lines, LANES), F32)
    corner = jnp.zeros((number * STRIP, LANES), F32)
    for j in range(z.rng):
        spread = marks((STRIP, LANES), lambda c, lane: lane == c + j * STRIP)
        at = z.rim_cols + (j * z.images + first) * z.lines
        side = side + dot(rim_ref[:STRIP, at : at + number * z.lines], spread, (0, 0))
        for i in range(z.az):
            at = z.rim_corners + (i * z.rng + j) * LANES
            turned = dot(rim_ref[:STRIP, at : at + LANES], spread, (0, 0)).astype(BF16)
            r = p % STRIP - az[i]
            wanted = jnp.where((r >= 0) & (r < HALF_AZ), r * z.images + first + p // STRIP, -1)
            put = near(wanted, lax.broadcasted_iota(jnp.int32, (number * STRIP, LANES), 1), 0)
            corner = corner + dot(put, turned)
    tile_ref[:, STRIP:, z.cols :] = side.astype(BF16).reshape(number, z.lines, LANES)
    tile_ref[:, :STRIP, z.cols :] = corner.astype(BF16).reshape(number, STRIP, LANES)


def split(x):
    high = x.astype(BF16)
    return high, (x - high.astype(F32)).astype(BF16)


def down_sums(z, x):
    half = STRIP // 2
    x = jnp.concatenate([x[half:], x[:half]], axis=0)
    top = half - HALF_AZ
    twos = x[top : top + z.lines + 3] + x[top + 1 : top + z.lines + 4]
    fours = twos[: z.lines + 1] + twos[2 : z.lines + 3]
    return fours[: z.lines] + x[half + HALF_AZ : half + HALF_AZ + z.lines]


def look_stats(z, tile, first, number, columns):
    powers, parts = [], []
    for d in range(first, first + number):
        re, im = tile[2 * d].astype(F32), tile[2 * d + 1].astype(F32)
        power = re * re + im * im
        powers.append(power[STRIP:, : z.cols])
        parts += split(power)
    sums = dot(jnp.concatenate(parts, axis=0), columns)
    for n, power in enumerate(powers):
        at = 2 * n * z.rows
        both = sums[at : at + z.rows] + sums[at + z.rows : at + 2 * z.rows]
        mean = down_sums(z, both) * (1.0 / LOOKS) + EPS
        yield first + n, power, mean, 1.0 / mean


def stats_kernel(z, x_ref, rim_ref, columns, tile_ref, mean_ref, inv_ref, log_ref, part_ref, bundle_ref):
    assemble(z, tile_ref, x_ref, rim_ref, 0, z.images)
    part = jnp.zeros((z.lines, z.cols), F32)
    for first in range(0, z.dates, BATCH):
        for d, power, mean, inv in look_stats(z, tile_ref, first, min(BATCH, z.dates - first), columns[...]):
            mean_ref[d] = mean
            inv_ref[d] = inv * (1.0 / LOOKS)
            log_ref[d] = jnp.log(mean)
            part = part + power * inv
    part = part.astype(BF16)
    part_ref[...] = part
    bundle_ref[:, : z.rim_width] = rim_ref[...]
    for i in range(z.lines // STRIP):
        at = z.rim_width + i * z.cols
        bundle_ref[:STRIP, at : at + z.cols] = part[i * STRIP : (i + 1) * STRIP]


def do_pairs(z, own, other, first_other, own_inv, own_log, other_inv, other_log, columns, lists, row, coh, log, emit=None):
    count = lists[row, z.slot_count]

    def pick(k):
        code = lists[row, jnp.minimum(k, count - 1)]
        return code // 65536, (code // 256) % 256, code % 256 - first_other

    def group(step, sent):
        picks = [pick(step * GROUP + g) for g in range(GROUP)]
        products = []
        for d, _, e in picks:
            a0, a1, b0, b1 = own[2 * d], own[2 * d + 1], other[2 * e], other[2 * e + 1]
            products += [a0 * b0 + a1 * b1, a1 * b0 - a0 * b1]
        sums = dot(jnp.concatenate(products, axis=0), columns)
        for g, (d, s, e) in enumerate(picks):
            at = 2 * g * z.rows
            re = down_sums(z, sums[at : at + z.rows])
            im = down_sums(z, sums[at + z.rows : at + 2 * z.rows])
            coh[d, s] = ((re * re + im * im) * (own_inv[d] * other_inv[e])).astype(BF16)
            log[d, s] = (own_log[d] - other_log[e]).astype(BF16)
        if emit is None:
            return sent
        following = (step + 1) * GROUP
        ready = jnp.where(following < count, pick(following)[0], z.dates)
        emit(sent, ready)
        return ready

    sent = lax.fori_loop(0, (count + GROUP - 1) // GROUP, group, 0)
    if emit is not None:
        emit(sent, z.dates)


def own_kernel(z, lists_ref, columns, tile, inv, log, coh, logr, lists, sem):
    take = pltpu.make_async_copy(lists_ref, lists, sem)
    take.start()
    take.wait()
    empty = jnp.zeros((z.lines, z.cols), BF16)

    def clear(k, _):
        code = lists[0, k]
        d, s = code // 65536, (code // 256) % 256
        coh[d, s] = empty
        logr[d, s] = empty
        return 0

    lax.fori_loop(0, lists[0, z.slot_count], clear, 0)
    do_pairs(z, tile, tile, 0, inv, log, inv, log, columns[...], lists, 1, coh, logr)


def cross_kernel(z, x_ref, rim_ref, lists_ref, columns, own, own_inv, own_log, coh_in, log_in, coh_out, log_out, coh_last, log_last, tile, inv, log, lists, coh, logr, sems):
    takes = [
        pltpu.make_async_copy(lists_ref, lists, sems.at[0]),
        pltpu.make_async_copy(coh_in, coh, sems.at[1]),
        pltpu.make_async_copy(log_in, logr, sems.at[2]),
    ]
    for take in takes:
        take.start()
    assemble(z, tile, x_ref, rim_ref, 0, z.images)
    for first in range(0, z.dates, BATCH):
        for d, _, mean, inverse in look_stats(z, tile, first, min(BATCH, z.dates - first), columns[...]):
            inv[d] = inverse * (1.0 / LOOKS)
            log[d] = jnp.log(mean)
    for take in takes:
        take.wait()

    spans = [(low, high - low) for low, high in zip((0,) + z.ends, z.ends)]

    def copies(low, number):
        span = pl.ds(low, number)
        return (
            pltpu.make_async_copy(coh.at[span], coh_out.at[span], sems.at[3]),
            pltpu.make_async_copy(logr.at[span], log_out.at[span], sems.at[3]),
        )

    def emit(sent, ready):
        for low, number in spans:

            @pl.when((sent < low + number) & (ready >= low + number))
            def _():
                for copy in copies(low, number):
                    copy.start()

    do_pairs(z, own, tile, z.dates, own_inv, own_log, inv, log, columns[...], lists, 2, coh, logr, emit)
    coh_last[...] = coh[z.ends[-1] :]
    log_last[...] = logr[z.ends[-1] :]
    for low, number in spans:
        for copy in copies(low, number):
            copy.wait()


def quegan_kernel(z, dates_total, rotated, coh_in, log_in, coh_last, log_last, mean, rim_ref, *refs):
    parts, (coh_out, log_out, out, stage, sems) = refs[:-5], refs[-5:]
    span = pl.ds(z.ends[-1], z.dates - z.ends[-1])
    copies = [
        pltpu.make_async_copy(coh_last, coh_out.at[span], sems.at[0]),
        pltpu.make_async_copy(log_last, log_out.at[span], sems.at[1]),
    ]
    half = z.dates // 2
    for low, number in ((0, half), (half, z.dates - half)):
        part = pl.ds(low, number)
        copies.append(pltpu.make_async_copy(stage.at[part], out.at[part], sems.at[len(copies)]))
    for copy in copies[:2]:
        copy.start()
    total = parts[0][...].astype(F32)
    for piece in parts[1:]:
        total = total + piece[...].astype(F32)
    if rotated:
        ats = [z.rim_width + i * z.cols for i in range(z.lines // STRIP)]
        total = total + jnp.concatenate([rim_ref[:STRIP, at : at + z.cols] for at in ats], axis=0).astype(F32)
    total = total * (1.0 / dates_total)
    for d in range(z.dates):
        stage[d] = mean[d] * total
        if d == half - 1:
            copies[2].start()
    copies[3].start()
    for copy in copies:
        copy.wait()


def vmem(n):
    return [pl.BlockSpec(memory_space=pltpu.VMEM)] * n


SMEM = pl.BlockSpec(memory_space=pltpu.SMEM)
HBM = pl.BlockSpec(memory_space=pltpu.HBM)
PARAMS = pltpu.CompilerParams(vmem_limit_bytes=32 * 1024 * 1024)
COST = pl.CostEstimate(flops=1, bytes_accessed=1, transcendentals=0)


def on_device(slc, lags):
    z = Sizes(slc, lags)
    shape = jax.ShapeDtypeStruct
    flat = slc.reshape(z.images * z.lines, z.cols)
    count = lax.axis_size("date")
    earlier = [(i, i - 1) for i in range(1, count)]
    later = lax.ppermute(flat, "date", earlier)
    packed = pl.pallas_call(
        lambda *refs: pack_kernel(z, *refs),
        out_shape=[shape((STRIP, HALF_AZ * z.cols), BF16)] * z.az
        + [shape((STRIP, z.images * z.lines), BF16)] * z.rng
        + [shape((STRIP, LANES), BF16)] * (z.az * z.rng)
        + [shape(flat.shape, BF16)],
        in_specs=[HBM],
        out_specs=vmem(z.az + z.rng + z.az * z.rng + 1),
        scratch_shapes=[pltpu.SemaphoreType.DMA((PARTS,))],
        compiler_params=PARAMS,
        cost_estimate=COST,
        name="pack",
    )(pltpu.with_memory_space_constraint(flat, pltpu.HBM))
    held = packed[-1]
    az, rng = sides("az", z.lines, HALF_AZ), sides("rng", z.cols, HALF_RG)

    lists_shape = (3, z.slot_count + 1)
    own_lists = pltpu.SMEM(lists_shape, jnp.int32)
    rim = [lax.ppermute(packed[i], "az", az[i][2]) for i in range(z.az)]
    lags, _ = lax.optimization_barrier((lags, packed[0]))
    columns, lists = pl.pallas_call(
        lambda *refs: prepare_kernel(z, *refs),
        out_shape=[shape((z.width, z.cols), BF16), shape(lists_shape, jnp.int32)],
        in_specs=[HBM],
        out_specs=vmem(2),
        scratch_shapes=[pltpu.SMEM(lags.shape, jnp.int32), own_lists, pltpu.SMEM((3,), jnp.int32)]
        + [pltpu.SemaphoreType.DMA],
        compiler_params=PARAMS,
        cost_estimate=COST,
        name="prepare",
    )(pltpu.with_memory_space_constraint(lags, pltpu.HBM))
    rim += [lax.ppermute(packed[z.az + j], "rng", rng[j][2]) for j in range(z.rng)]
    az_count = lax.axis_size("az")
    for i in range(z.az):
        for j in range(z.rng):
            pairs = [(a * az_count + b, c * az_count + d) for a, c in rng[j][2] for b, d in az[i][2]]
            rim.append(lax.ppermute(packed[z.az + z.rng + i * z.rng + j], ("rng", "az"), pairs))
    rim, _ = lax.optimization_barrier((rim, columns))
    rim = jnp.concatenate(rim, axis=1)
    field = shape((z.dates, z.lines, z.cols), F32)
    out = shape((z.dates, z.slots, z.lines, z.cols), BF16)
    own, mean, inv, log, part, bundle = pl.pallas_call(
        lambda *refs: stats_kernel(z, *refs),
        out_shape=[shape((z.images, z.rows, z.width), BF16), field, field, field, shape((z.lines, z.cols), BF16)]
        + [shape((rim.shape[0], z.rim_width + z.cols * (z.lines // STRIP)), BF16)],
        in_specs=vmem(3),
        out_specs=vmem(6),
        compiler_params=PARAMS,
        cost_estimate=COST,
        name="stats",
    )(held, rim, columns)

    rotated = 2 < count <= 4
    if rotated:
        later_rim = lax.ppermute(bundle, "date", [(i, (i - 1) % count) for i in range(count)])
        parts = [part]
        for k in range(2, count):
            parts.append(lax.ppermute(part, "date", [(i, (i - k) % count) for i in range(count)]))
    else:
        later_rim = lax.ppermute(rim, "date", earlier)
        parts = [lax.psum(part, "date")]

    coherence, log_ratio = pl.pallas_call(
        lambda *refs: own_kernel(z, *refs),
        out_shape=[out, out],
        in_specs=vmem(5),
        out_specs=vmem(2),
        scratch_shapes=[own_lists, pltpu.SemaphoreType.DMA],
        compiler_params=PARAMS,
        cost_estimate=COST,
        name="own",
    )(lists, columns, own, inv, log)
    other, held_out = pltpu.VMEM(field.shape, F32), pltpu.VMEM(out.shape, BF16)
    last = shape((z.dates - z.ends[-1],) + out.shape[1:], BF16)
    coherence, log_ratio, coh_last, log_last = pl.pallas_call(
        lambda *refs: cross_kernel(z, *refs),
        out_shape=[out, out, last, last],
        in_specs=vmem(9),
        out_specs=[HBM] * 2 + vmem(2),
        scratch_shapes=[pltpu.VMEM((z.images, z.rows, z.width), BF16), other, other, own_lists, held_out, held_out]
        + [pltpu.SemaphoreType.DMA((4,))],
        compiler_params=PARAMS,
        cost_estimate=COST,
        name="cross",
    )(later, later_rim, lists, columns, own, inv, log, coherence, log_ratio)
    return pl.pallas_call(
        lambda *refs: quegan_kernel(z, z.dates * count, rotated, *refs),
        out_shape=(out, out, field),
        in_specs=[HBM] * 2 + vmem(4 + len(parts)),
        out_specs=(HBM, HBM, HBM),
        scratch_shapes=[pltpu.VMEM(field.shape, F32), pltpu.SemaphoreType.DMA((4,))],
        input_output_aliases={0: 0, 1: 1},
        compiler_params=PARAMS,
        cost_estimate=COST,
        name="quegan",
    )(coherence, log_ratio, coh_last, log_last, mean, later_rim, *parts)


def solution(mesh):
    return jax.shard_map(
        on_device,
        mesh=mesh,
        in_specs=(P(("slab", "date"), None, "az", "rng"), P("date", None)),
        out_specs=(
            P(("slab", "date"), None, "az", "rng"),
            P(("slab", "date"), None, "az", "rng"),
            P(("slab", "date"), "az", "rng"),
        ),
        check_vma=False,
    )
```
